128 devices in a mesh: slab: 16 (over x, z), member: 8 (over y, core).
Axes of the slice: x: 4, y: 4, z: 4, core: 2. Of those that a mesh axis runs over, the one named last changes fastest.
Arguments:
- embeddings: bfloat16 [131072, 768], P(('slab', 'member')), may hold values from -6 to 6
- cluster_ids: int32 [131072], P(('slab', 'member')), may hold values from 0 to 63, never falling along the last dimension, each value on 1 to 4097 neighbouring positions
- keep_mask: int32 [131072], P(('slab', 'member')), may hold values 0 or 1
Outputs:
- highest: float32 [131072], P(('slab', 'member'))
The draws below stay inside these ranges and needn't reach their ends.
Inputs may be any that keep to these rules, and one draw needn't show every extreme that they name: `cluster_ids`: never falling along the rows; each cluster is a run of 1 to 4097 consecutive rows, and some cluster has exactly 4097 rows.
All inputs are finite; a program needn't handle non-finite values. No bound on the sum of `keep_mask` on one device may be relied on, other than what follows from the above.
Results may differ from the reference program's by a relative error of at most 0.0013.
Values may be sent and summed in bfloat16 or wider, within the bound.
A program may use at most 64 MiB of HBM per device.

```python
import math
import jax
import jax.numpy as jnp
import numpy as np
from jax import lax

D = 768
ROWS_DEV = 1024
REACH = 4
ROWS = 131072
MOST = 4097
CLUSTERS = 64
N_SLAB = 16
N_MEMBER = 8


def plant(drawn, rng, low, largest):
    place = [jax.random.randint(jax.random.fold_in(rng, axis), (), 0, length) for axis, length in enumerate(drawn.shape)]
    main_axis = drawn.shape.index(max(drawn.shape))
    next_to = place[:main_axis] + [(place[main_axis] + 1) % drawn.shape[main_axis]] + place[main_axis + 1:]
    return drawn.at[tuple(place)].set(low).at[tuple(next_to)].set(largest)


def levels(key, extent, split, least, largest):
    level, own = 1.0, jax.random.fold_in(key, 6)
    for dim, parts in split:
        draws = jnp.exp(jax.random.uniform(jax.random.fold_in(own, dim), (parts,), jnp.float32, least / len(split), largest / len(split)))
        level = level * jnp.repeat(draws, extent[dim] // parts).reshape([-1 if axis == dim else 1 for axis in range(len(extent))])
    return level


def split_up(amount, total, most, skew):
    portions = [(1 << 20) // math.isqrt(rank ** skew) + 1 for rank in range(2, amount + 1)]
    rest, counts = total - most - (amount - 1), [1] * (amount - 1)
    while rest > 0:
        movable = [i for i in range(amount - 1) if counts[i] < most]
        pool, remaining = sum([portions[i] for i in movable]), rest
        for i in movable:
            extra = min(most - counts[i], max(1, remaining * portions[i] // pool), rest)
            counts[i] = counts[i] + extra
            rest = rest - extra
    return np.array([most] + counts)


def ragged_sizes(rng, number_of, total, bound, slope):
    if number_of == 2:
        one = jax.random.randint(rng, (), max(1, total - bound), min(bound, total - 1) + 1)
        return jnp.stack([one, total - one])
    sizes = jnp.asarray(split_up(number_of, total, bound, slope), jnp.int32)
    couples = (number_of - 1) // 2
    donor, taker = sizes[1:1 + 2 * couples:2], sizes[2:2 + 2 * couples:2]
    margin = jnp.minimum(donor - 1, bound - taker)
    shifted = jax.random.randint(jax.random.fold_in(rng, 1), (couples,), 0, 1 << 20) % (margin + 1)
    sizes = sizes.at[1:1 + 2 * couples:2].set(donor - shifted).at[2:2 + 2 * couples:2].set(taker + shifted)
    return sizes[jax.random.permutation(jax.random.fold_in(rng, 2), number_of)]


def centred(key, shape, scale, most, cuts=(), held_as=jnp.bfloat16):
    values = jax.random.normal(key, shape, jnp.float32) * scale
    if len(cuts) > 0:
        values = levels(key, shape, cuts, -0.22, 0.18) * values
    return jnp.clip(values, min=-most, max=most).astype(held_as)


def setup_inputs(seed: int = 0) -> dict:
    streams_of = jax.random.split(jax.random.key(seed), 4)
    embeddings = centred(streams_of[0], (ROWS, D), 1.0, 6.0, ((0, 128),))
    cluster_ids = jnp.searchsorted(jnp.cumsum(ragged_sizes(streams_of[1], CLUSTERS, ROWS, MOST, 2)), jnp.arange(ROWS), side="right").astype(jnp.int32)
    keep_mask = plant((jax.random.randint(streams_of[2], (ROWS,), 0, 8) < 7).astype(jnp.int32), jax.random.fold_in(streams_of[2], 1), 0, 1)
    return {"embeddings": embeddings, "cluster_ids": cluster_ids, "keep_mask": keep_mask}


def reference(embeddings, cluster_ids, keep_mask):
    values = embeddings.astype(jnp.float32)
    unit_rows = (values * lax.rsqrt(lax.optimization_barrier(jnp.sum(values * values, axis=1, keepdims=True)) + 1e-06)).astype(jnp.bfloat16)
    labels = jnp.where(keep_mask == 1, cluster_ids, -1).astype(jnp.int32)
    blocks = N_SLAB * N_MEMBER
    unit_blocks = unit_rows.reshape(blocks, ROWS_DEV, D)
    id_blocks = cluster_ids.reshape(blocks, ROWS_DEV)
    label_blocks = labels.reshape(blocks, ROWS_DEV)
    diagonal = jnp.eye(ROWS_DEV, dtype=bool)

    def block_max(block):
        own_rows = unit_blocks[block]
        own_ids = id_blocks[block]
        highest = jnp.full((ROWS_DEV,), -1.0, jnp.float32)
        for offset in range(-REACH, REACH + 1):
            other = block + offset
            inside = (other >= 0) & (other < blocks)
            clipped = jnp.clip(other, 0, blocks - 1).astype(jnp.int32)
            other_rows = unit_blocks[clipped]
            other_labels = label_blocks[clipped]
            other_ids = id_blocks[clipped]
            shares = inside & (other_ids[0] <= own_ids[-1]) & (other_ids[-1] >= own_ids[0])

            def compute(operands):
                scores = jnp.dot(own_rows, other_rows.T, preferred_element_type=jnp.float32)
                matches = own_ids[:, None] == other_labels[None, :]
                if offset == 0:
                    matches = matches & jnp.logical_not(diagonal)
                return lax.optimization_barrier(jnp.max(jnp.where(matches, scores, -1.0), axis=1))

            def skipped(operands):
                return jnp.full((ROWS_DEV,), -1.0, jnp.float32)
            highest = jnp.maximum(highest, lax.cond(shares, compute, skipped, 0))
        return highest
    result = lax.map(block_max, jnp.arange(blocks, dtype=jnp.int32))
    return result.reshape(ROWS)
```

```python
import functools

import jax
import jax.numpy as jnp
from jax import lax
from jax.experimental import pallas as pl
from jax.experimental.pallas import tpu as pltpu
from jax.sharding import PartitionSpec as P

MESH = pl.DeviceIdType.MESH
OWN, A, B, C = 0, 1, 2, 3
LANES = 128
OUT = -4.0


def kernel(n_slab, n_member, x_ref, ids_ref, keep_ref, out_ref, raw, blk, tags, pres, qacc, msg, got,
           load_sem, send_sem, recv_sem, tag_send, tag_recv, msg_send, msg_recv):
    rows, width = raw.shape
    chunks = rows // LANES
    count = n_slab * n_member
    slab, member = lax.axis_index("slab"), lax.axis_index("member")
    core = lax.rem(member, 2)
    place = slab * n_member + member

    def device(at):
        at = lax.rem(at + count, count)
        return (lax.div(at, n_member), lax.rem(at, n_member))

    first = device(place - 2 + 4 * core)
    second = device(place + 2 - 4 * core)
    sibling = (slab, member + 1 - 2 * core)
    above, below = device(place + 1), device(place - 1)

    barrier = pltpu.get_barrier_semaphore()
    for other in (first, second, above, below):
        pl.semaphore_signal(barrier, inc=1, device_id=other, device_id_type=MESH)

    def part(t):
        return pl.ds(pl.multiple_of(t * LANES, LANES), LANES)

    def load(t):
        return pltpu.make_async_copy(x_ref.at[part(t)], raw.at[part(t)], load_sem.at[t])

    def send(src_slot, dst_slot, t, target):
        return pltpu.make_async_remote_copy(
            src_ref=blk.at[src_slot, part(t)], dst_ref=blk.at[dst_slot, part(t)],
            send_sem=send_sem.at[dst_slot, t], recv_sem=recv_sem.at[dst_slot, t],
            device_id=target, device_id_type=MESH)

    def send_tags(src_slot, dst_slot, target):
        return pltpu.make_async_remote_copy(
            src_ref=tags.at[src_slot], dst_ref=tags.at[dst_slot], send_sem=tag_send.at[dst_slot],
            recv_sem=tag_recv.at[dst_slot], device_id=target, device_id_type=MESH)

    for t in range(chunks):
        load(t).start()
    tags[OWN, 0:chunks] = ids_ref[...]
    tags[OWN, chunks:2 * chunks] = jnp.where(keep_ref[...] == 1, ids_ref[...], -1)
    pres[...] = jnp.full(pres.shape, OUT, jnp.float32)
    qacc[...] = jnp.full(qacc.shape, OUT, jnp.float32)

    def normalise(t):
        load(t).wait()
        values = raw[part(t), :].astype(jnp.float32)
        scale = lax.rsqrt(jnp.sum(values * values, axis=1, keepdims=True) + 1e-06)
        blk[OWN, part(t), :] = (values * scale).astype(jnp.bfloat16)

    normalise(0)
    pl.semaphore_wait(barrier, 4)
    send_tags(OWN, A, first).start()
    send_tags(OWN, B, second).start()
    send(OWN, A, 0, first).start()

    def prepare(t, _):
        normalise(t)
        send(OWN, A, t, first).start()
        return 0

    lax.fori_loop(1, chunks, prepare, 0)

    def row(slot, t):
        return tags[slot, pl.ds(t, 1), :]

    def columns(values):
        return jnp.broadcast_to(values, (LANES, LANES)).T

    def fold(values):
        return jnp.max(values.reshape(LANES // 8, 8, LANES), axis=0)

    def scores(p, q_slot, n):
        q = blk[q_slot, 2 * n * LANES:2 * (n + 1) * LANES, :]
        return lax.dot_general(p, q, (((1,), (1,)), ((), ())), preferred_element_type=jnp.float32)

    def own_step(t, _):
        p = blk[OWN, part(t), :]
        labels = columns(row(OWN, chunks + t).astype(jnp.float32))
        down = lax.broadcasted_iota(jnp.int32, (LANES, LANES), 0) + t * LANES
        along = lax.broadcasted_iota(jnp.int32, (LANES, LANES), 1)
        for n in range(chunks // 2):
            s = scores(p, OWN, n)
            for h in range(2):
                tile = 2 * n + h
                ids = row(OWN, tile).astype(jnp.float32)
                hits = (labels == ids) & (down != along + tile * LANES)
                top = fold(jnp.where(hits, s[:, h * LANES:(h + 1) * LANES], OUT))
                at = (0, slice(None), slice(tile * LANES, (tile + 1) * LANES))
                qacc[at] = jnp.maximum(qacc[at], top)
        return 0

    def shared(slot):
        low, high = tags[slot, 0:1, 0:1], tags[slot, chunks - 1:chunks, LANES - 1:LANES]
        if slot == C:
            return low
        return jnp.where(core == (0 if slot == A else 1), low, high)

    def pair_step(p_slot, q_slot, t, cluster, q_at):
        p = blk[p_slot, part(t), :]
        p_bias = columns(jnp.where(row(p_slot, chunks + t) == cluster, 0.0, OUT))
        best = jnp.full((LANES, LANES), OUT, jnp.float32)
        for n in range(chunks // 2):
            s = scores(p, q_slot, n)
            for h in range(2):
                tile = 2 * n + h
                one = s[:, h * LANES:(h + 1) * LANES]
                q_bias = jnp.where(row(q_slot, chunks + tile) == cluster, 0.0, OUT)
                best = jnp.maximum(best, one + q_bias)
                at = (q_at, slice(None), slice(tile * LANES, (tile + 1) * LANES))
                qacc[at] = jnp.maximum(qacc[at], fold(one + p_bias))
        at = (p_slot - 1, slice(None), part(t))
        pres[at] = jnp.maximum(pres[at], fold(best.T))

    lax.fori_loop(0, chunks, own_step, 0)

    c_source = jnp.where(core == 0, A, OWN)
    send_tags(OWN, A, first).wait()
    send_tags(OWN, B, second).wait()
    send_tags(c_source, C, sibling).start()
    send_tags(c_source, C, sibling).wait()
    s_a, s_b, s_c = shared(A), shared(B), shared(C)

    def first_step(t, _):
        send(OWN, A, t, first).wait_recv()
        send(c_source, C, t, sibling).start()
        pair_step(A, OWN, t, s_a, 1)
        send(c_source, C, t, sibling).wait_recv()
        pair_step(C, OWN, t, s_c, 2)
        send(OWN, A, t, first).wait_send()

        @pl.when(t == chunks - 2)
        def _():
            send(OWN, B, 0, second).start()
            send(OWN, B, 1, second).start()

        return 0

    lax.fori_loop(0, chunks, first_step, 0)
    for t in range(2, chunks):
        send(OWN, B, t, second).start()

    def second_step(t, _):
        @pl.when(core == 1)
        def _():
            pair_step(C, A, t, s_c, 4)

        send(OWN, B, t, second).wait_recv()
        pair_step(B, A, t, s_b, 3)

        @pl.when(core == 0)
        def _():
            pair_step(B, C, t, s_b, 4)

        return 0

    lax.fori_loop(0, chunks, second_step, 0)

    def masked(slot, tile, cluster, values):
        lanes = slice(tile * LANES, (tile + 1) * LANES)
        top = jnp.max(values[:, lanes], axis=0, keepdims=True)
        return jnp.where(row(slot, tile) == cluster, top, -1.0)

    def message(which, target):
        return pltpu.make_async_remote_copy(
            src_ref=msg.at[which], dst_ref=got.at[which], send_sem=msg_send.at[which],
            recv_sem=msg_recv.at[which], device_id=target, device_id_type=MESH)

    targets = (second, first, above)
    extra = qacc[4]
    for tile in range(chunks):
        msg[0, tile:tile + 1, :] = jnp.maximum(
            jnp.maximum(masked(A, tile, s_a, pres[0]), masked(A, tile, s_b, qacc[3])),
            jnp.where(core == 1, masked(A, tile, s_c, extra), -1.0))
        msg[1, tile:tile + 1, :] = masked(B, tile, s_b, pres[1])
        msg[2, tile:tile + 1, :] = jnp.maximum(
            masked(C, tile, s_c, pres[2]), jnp.where(core == 0, masked(C, tile, s_b, extra), -1.0))
    for which in range(3):
        message(which, targets[which]).start()
    for tile in range(chunks):
        lanes = slice(tile * LANES, (tile + 1) * LANES)
        own = jnp.max(qacc[0, :, lanes], axis=0, keepdims=True)
        out_ref[tile:tile + 1, :] = jnp.maximum(
            jnp.maximum(own, -1.0),
            jnp.maximum(masked(OWN, tile, s_a, qacc[1]), masked(OWN, tile, s_c, qacc[2])))
    for t in range(chunks):
        send(OWN, B, t, second).wait_send()
        send(c_source, C, t, sibling).wait_send()
    for which in range(3):
        message(which, targets[which]).wait()
    out_ref[...] = jnp.maximum(jnp.maximum(out_ref[...], got[0]), jnp.maximum(got[1], got[2]))


def shards(n_slab, n_member, embeddings, cluster_ids, keep_mask):
    rows, width = embeddings.shape
    chunks = rows // LANES
    vmem = pl.BlockSpec(memory_space=pltpu.VMEM)
    highest = pl.pallas_call(
        functools.partial(kernel, n_slab, n_member),
        out_shape=jax.ShapeDtypeStruct((chunks, LANES), jnp.float32),
        in_specs=[pl.BlockSpec(memory_space=pltpu.HBM), vmem, vmem],
        out_specs=vmem,
        scratch_shapes=[
            pltpu.VMEM((rows, width), jnp.bfloat16),
            pltpu.VMEM((4, rows, width), jnp.bfloat16),
            pltpu.VMEM((4, 2 * chunks, LANES), jnp.int32),
            pltpu.VMEM((3, 8, rows), jnp.float32),
            pltpu.VMEM((5, 8, rows), jnp.float32),
            pltpu.VMEM((3, chunks, LANES), jnp.float32),
            pltpu.VMEM((3, chunks, LANES), jnp.float32),
            pltpu.SemaphoreType.DMA((chunks,)),
            pltpu.SemaphoreType.DMA((4, chunks)),
            pltpu.SemaphoreType.DMA((4, chunks)),
            pltpu.SemaphoreType.DMA((4,)),
            pltpu.SemaphoreType.DMA((4,)),
            pltpu.SemaphoreType.DMA((3,)),
            pltpu.SemaphoreType.DMA((3,)),
        ],
        compiler_params=pltpu.CompilerParams(
            collective_id=0, has_side_effects=True, vmem_limit_bytes=40 << 20),
    )(embeddings, cluster_ids.reshape(chunks, LANES), keep_mask.reshape(chunks, LANES))
    return highest.reshape(rows)


def solution(mesh):
    placed = (P(("slab", "member"), None), P(("slab", "member")), P(("slab", "member")))
    return jax.shard_map(
        functools.partial(shards, mesh.shape["slab"], mesh.shape["member"]),
        mesh=mesh, in_specs=placed, out_specs=P(("slab", "member")), check_vma=False,
    )
```

```python
import functools

import jax
import jax.numpy as jnp
from jax import lax
from jax.experimental import pallas as pl
from jax.experimental.pallas import tpu as pltpu
from jax.sharding import PartitionSpec as P

MESH = pl.DeviceIdType.MESH
OWN, A, B, C = 0, 1, 2, 3
LANES = 128
OUT = -4.0


def kernel(n_slab, n_member, x_ref, ids_ref, keep_ref, out_ref, raw, blk, tags, pres, qacc, msg, got,
           load_sem, send_sem, recv_sem, tag_send, tag_recv, msg_send, msg_recv):
    rows, width = raw.shape
    chunks = rows // LANES
    count = n_slab * n_member
    slab, member = lax.axis_index("slab"), lax.axis_index("member")
    core = lax.rem(member, 2)
    place = slab * n_member + member
    chip = lax.div(place, 2)
    has_down, has_up = chip > 0, chip < count // 2 - 1
    even, odd = core == 0, core == 1

    def device(at):
        at = jnp.clip(at, 0, count - 1)
        return (lax.div(at, n_member), lax.rem(at, n_member))

    first, second = device(place - 2 + 4 * core), device(place + 2 - 4 * core)
    has_first = (even & has_down) | (odd & has_up)
    has_second = (even & has_up) | (odd & has_down)
    has_a, has_b, has_c = has_second, has_first, even | has_up
    gives_c = odd | has_up
    c_source = jnp.where(even, A, OWN)
    sibling = (slab, member + 1 - 2 * core)
    above, below = device(place + 1), device(place - 1)

    barrier = pltpu.get_barrier_semaphore()
    partners = ((has_first, first), (has_second, second), (place < count - 1, above), (place > 0, below))
    for there, other in partners:
        @pl.when(there)
        def _():
            pl.semaphore_signal(barrier, inc=1, device_id=other, device_id_type=MESH)

    def part(t):
        return pl.ds(pl.multiple_of(t * LANES, LANES), LANES)

    def pair_of_parts(t):
        return pl.ds(pl.multiple_of(t * 2 * LANES, 2 * LANES), 2 * LANES)

    def load(t):
        return pltpu.make_async_copy(x_ref.at[part(t)], raw.at[part(t)], load_sem.at[t])

    def send(src_slot, dst_slot, t, target):
        return pltpu.make_async_remote_copy(
            src_ref=blk.at[src_slot, part(t)], dst_ref=blk.at[dst_slot, part(t)],
            send_sem=send_sem.at[dst_slot, t], recv_sem=recv_sem.at[dst_slot, t],
            device_id=target, device_id_type=MESH)

    def send_tags(src_slot, dst_slot, target):
        return pltpu.make_async_remote_copy(
            src_ref=tags.at[src_slot], dst_ref=tags.at[dst_slot], send_sem=tag_send.at[dst_slot],
            recv_sem=tag_recv.at[dst_slot], device_id=target, device_id_type=MESH)

    load_ids = pltpu.make_async_copy(ids_ref, tags.at[OWN, 0:chunks], load_sem.at[chunks])
    load_keep = pltpu.make_async_copy(keep_ref, tags.at[OWN, chunks:2 * chunks], load_sem.at[chunks + 1])
    load(0).start()
    load_ids.start()
    load_keep.start()
    for t in range(1, chunks):
        load(t).start()
    for slot, there in ((A, has_a), (B, has_b), (C, has_c)):
        @pl.when(jnp.logical_not(there))
        def _():
            tags[slot] = jnp.full(tags.shape[1:], -2, jnp.int32)
    pres[...] = jnp.full(pres.shape, OUT, jnp.float32)
    qacc[...] = jnp.full(qacc.shape, OUT, jnp.float32)

    def normalise(t):
        load(t).wait()
        values = raw[part(t), :].astype(jnp.float32)
        scale = lax.rsqrt(jnp.sum(values * values, axis=1, keepdims=True) + 1e-06)
        blk[OWN, part(t), :] = (values * scale).astype(jnp.bfloat16)

    normalise(0)
    load_ids.wait()
    load_keep.wait()
    tags[OWN, chunks:2 * chunks] = jnp.where(tags[OWN, chunks:2 * chunks] == 1, tags[OWN, 0:chunks], -1)
    pl.semaphore_wait(barrier, sum(there.astype(jnp.int32) for there, _ in partners))

    @pl.when(has_first)
    def _():
        send(OWN, A, 0, first).start()
        send_tags(OWN, A, first).start()

    @pl.when(has_second)
    def _():
        send_tags(OWN, B, second).start()

    def prepare(t, _):
        normalise(t)

        @pl.when(has_first)
        def _():
            send(OWN, A, t, first).start()

        return 0

    lax.fori_loop(1, chunks, prepare, 0)

    def row(slot, t):
        return tags[slot, pl.ds(t, 1), :]

    def columns(values):
        return jnp.broadcast_to(values, (LANES, LANES)).T

    def fold(values):
        return jnp.max(values.reshape(values.shape[0] // 8, 8, LANES), axis=0)

    def scores(p, q_slot, n):
        q = blk[q_slot, 2 * n * LANES:2 * (n + 1) * LANES, :]
        return lax.dot_general(p, q, (((1,), (1,)), ((), ())), preferred_element_type=jnp.float32)

    def own_step(t, _):
        p = blk[OWN, pair_of_parts(t), :]
        labels = jnp.concatenate(
            [columns(row(OWN, chunks + 2 * t + i).astype(jnp.float32)) for i in range(2)], axis=0)
        down = lax.broadcasted_iota(jnp.int32, (2 * LANES, LANES), 0) + t * 2 * LANES
        along = lax.broadcasted_iota(jnp.int32, (2 * LANES, LANES), 1)
        for n in range(chunks // 2):
            s = scores(p, OWN, n)
            for h in range(2):
                tile = 2 * n + h
                ids = row(OWN, tile).astype(jnp.float32)
                hits = (labels == ids) & (down != along + tile * LANES)
                top = fold(jnp.where(hits, s[:, h * LANES:(h + 1) * LANES], OUT))
                at = (0, slice(None), slice(tile * LANES, (tile + 1) * LANES))
                qacc[at] = jnp.maximum(qacc[at], top)
        return 0

    def shared(slot):
        low, high = tags[slot, 0:1, 0:1], tags[slot, chunks - 1:chunks, LANES - 1:LANES]
        if slot == C:
            return low
        return jnp.where(core == (0 if slot == A else 1), low, high)

    def pair_step(p_slot, q_slot, t, size, cluster, q_at):
        p = blk[p_slot, pair_of_parts(t) if size == 2 else part(t), :]
        p_bias = [columns(jnp.where(row(p_slot, chunks + size * t + i) == cluster, 0.0, OUT)) for i in range(size)]
        p_bias = jnp.concatenate(p_bias, axis=0) if size > 1 else p_bias[0]
        best = jnp.full((size * LANES, LANES), OUT, jnp.float32)
        for n in range(chunks // 2):
            s = scores(p, q_slot, n)
            for h in range(2):
                tile = 2 * n + h
                one = s[:, h * LANES:(h + 1) * LANES]
                q_bias = jnp.where(row(q_slot, chunks + tile) == cluster, 0.0, OUT)
                best = jnp.maximum(best, one + q_bias)
                at = (q_at, slice(None), slice(tile * LANES, (tile + 1) * LANES))
                qacc[at] = jnp.maximum(qacc[at], fold(one + p_bias))
        for i in range(size):
            at = (p_slot - 1, slice(None), part(size * t + i))
            pres[at] = jnp.maximum(pres[at], fold(best[i * LANES:(i + 1) * LANES].T))

    lax.fori_loop(0, chunks // 2, own_step, 0)

    @pl.when(has_first)
    def _():
        send_tags(OWN, A, first).wait_send()

    @pl.when(has_second)
    def _():
        send_tags(OWN, B, second).wait_send()

    @pl.when(has_a)
    def _():
        send_tags(OWN, A, first).wait_recv()

    @pl.when(has_b)
    def _():
        send_tags(OWN, B, second).wait_recv()

    @pl.when(gives_c)
    def _():
        send_tags(c_source, C, sibling).start()
        send_tags(c_source, C, sibling).wait_send()

    @pl.when(has_c)
    def _():
        send_tags(c_source, C, sibling).wait_recv()

    s_a, s_b, s_c = shared(A), shared(B), shared(C)
    early = 2

    def first_step(t, _):
        @pl.when((t == chunks // 2 - 1) & has_first)
        def _():
            for i in range(chunks - 2):
                send(OWN, A, i, first).wait_send()

        @pl.when((t == chunks // 2 - 1) & has_second)
        def _():
            for i in range(early):
                send(OWN, B, i, second).start()

        for i in range(2):
            @pl.when(has_a)
            def _():
                send(OWN, A, 2 * t + i, first).wait_recv()

            @pl.when(gives_c)
            def _():
                send(c_source, C, 2 * t + i, sibling).start()

        @pl.when((t == chunks // 2 - 1) & has_second)
        def _():
            for i in range(early, chunks):
                send(OWN, B, i, second).start()

        @pl.when(has_a)
        def _():
            pair_step(A, OWN, t, 2, s_a, 1)

        @pl.when(has_c)
        def _():
            for i in range(2):
                send(c_source, C, 2 * t + i, sibling).wait_recv()
            pair_step(C, OWN, t, 2, s_c, 2)

        return 0

    lax.fori_loop(0, chunks // 2, first_step, 0)

    @pl.when(odd & has_a & has_c)
    def _():
        def extra_step(t, _):
            pair_step(C, A, t, 2, s_c, 4)
            return 0

        lax.fori_loop(0, chunks // 2, extra_step, 0)

    def second_step(t, _):
        @pl.when(has_b)
        def _():
            send(OWN, B, t, second).wait_recv()

        @pl.when(has_a & has_b)
        def _():
            pair_step(B, A, t, 1, s_b, 3)

        @pl.when(even & has_b)
        def _():
            pair_step(B, C, t, 1, s_b, 4)

        return 0

    lax.fori_loop(0, chunks, second_step, 0)

    def masked(slot, tile, cluster, values):
        lanes = slice(tile * LANES, (tile + 1) * LANES)
        top = jnp.max(values[:, lanes], axis=0, keepdims=True)
        return jnp.where(row(slot, tile) == cluster, top, -1.0)

    def message(which, target):
        return pltpu.make_async_remote_copy(
            src_ref=msg.at[which], dst_ref=got.at[which], send_sem=msg_send.at[which],
            recv_sem=msg_recv.at[which], device_id=target, device_id_type=MESH)

    messages = ((has_a, second, has_first), (has_b, first, has_second), (has_c, above, odd | has_down))
    extra = qacc[4]
    for tile in range(chunks):
        msg[0, tile:tile + 1, :] = jnp.maximum(
            jnp.maximum(masked(A, tile, s_a, pres[0]), masked(A, tile, s_b, qacc[3])),
            jnp.where(odd, masked(A, tile, s_c, extra), -1.0))
        msg[1, tile:tile + 1, :] = masked(B, tile, s_b, pres[1])
        msg[2, tile:tile + 1, :] = jnp.maximum(
            masked(C, tile, s_c, pres[2]), jnp.where(even, masked(C, tile, s_b, extra), -1.0))
    for which, (gives, target, _) in enumerate(messages):
        @pl.when(gives)
        def _():
            message(which, target).start()
    for tile in range(chunks):
        lanes = slice(tile * LANES, (tile + 1) * LANES)
        own = jnp.max(qacc[0, :, lanes], axis=0, keepdims=True)
        out_ref[tile:tile + 1, :] = jnp.maximum(
            jnp.maximum(own, -1.0),
            jnp.maximum(masked(OWN, tile, s_a, qacc[1]), masked(OWN, tile, s_c, qacc[2])))

    @pl.when(has_first)
    def _():
        for t in range(chunks - 2, chunks):
            send(OWN, A, t, first).wait_send()

    @pl.when(has_second)
    def _():
        for t in range(chunks):
            send(OWN, B, t, second).wait_send()

    @pl.when(gives_c)
    def _():
        for t in range(chunks):
            send(c_source, C, t, sibling).wait_send()

    for which, (gives, target, gets) in enumerate(messages):
        @pl.when(gives)
        def _():
            message(which, target).wait_send()

        @pl.when(gets)
        def _():
            message(which, target).wait_recv()
            out_ref[...] = jnp.maximum(out_ref[...], got[which])


def shards(n_slab, n_member, embeddings, cluster_ids, keep_mask):
    rows, width = embeddings.shape
    chunks = rows // LANES
    highest = pl.pallas_call(
        functools.partial(kernel, n_slab, n_member),
        out_shape=jax.ShapeDtypeStruct((chunks, LANES), jnp.float32),
        in_specs=[pl.BlockSpec(memory_space=pltpu.HBM)] * 3,
        out_specs=pl.BlockSpec(memory_space=pltpu.VMEM),
        scratch_shapes=[
            pltpu.VMEM((rows, width), jnp.bfloat16),
            pltpu.VMEM((4, rows, width), jnp.bfloat16),
            pltpu.VMEM((4, 2 * chunks, LANES), jnp.int32),
            pltpu.VMEM((3, 8, rows), jnp.float32),
            pltpu.VMEM((5, 8, rows), jnp.float32),
            pltpu.VMEM((3, chunks, LANES), jnp.float32),
            pltpu.VMEM((3, chunks, LANES), jnp.float32),
            pltpu.SemaphoreType.DMA((chunks + 2,)),
            pltpu.SemaphoreType.DMA((4, chunks)),
            pltpu.SemaphoreType.DMA((4, chunks)),
            pltpu.SemaphoreType.DMA((4,)),
            pltpu.SemaphoreType.DMA((4,)),
            pltpu.SemaphoreType.DMA((3,)),
            pltpu.SemaphoreType.DMA((3,)),
        ],
        compiler_params=pltpu.CompilerParams(
            collective_id=0, has_side_effects=True, vmem_limit_bytes=60 << 20),
    )(embeddings, cluster_ids.reshape(chunks, LANES), keep_mask.reshape(chunks, LANES))
    return highest.reshape(rows)


def solution(mesh):
    placed = (P(("slab", "member"), None), P(("slab", "member")), P(("slab", "member")))
    return jax.shard_map(
        functools.partial(shards, mesh.shape["slab"], mesh.shape["member"]),
        mesh=mesh, in_specs=placed, out_specs=P(("slab", "member")), check_vma=False,
    )
```

```python
import functools

import jax
import jax.numpy as jnp
from jax import lax
from jax.experimental import pallas as pl
from jax.experimental.pallas import tpu as pltpu
from jax.sharding import PartitionSpec as P

MESH = pl.DeviceIdType.MESH
OWN, A, B, C = 0, 1, 2, 3
LANES = 128
GROUP = 2 * LANES
LEAD = 4
OUT = -4.0


def kernel(n_slab, n_member, x_ref, ids_ref, keep_ref, out_ref, raw, blk, tags, pres, qacc, msg, got,
           load_sem, send_sem, recv_sem, tag_send, tag_recv, msg_send, msg_recv):
    rows, width = raw.shape
    chunks, groups = rows // LANES, rows // GROUP
    count = n_slab * n_member
    slab, member = lax.axis_index("slab"), lax.axis_index("member")
    core = lax.rem(member, 2)
    place = slab * n_member + member
    chip = lax.div(place, 2)
    has_down, has_up = chip > 0, chip < count // 2 - 1
    even, odd = core == 0, core == 1

    def device(at):
        at = jnp.clip(at, 0, count - 1)
        return (lax.div(at, n_member), lax.rem(at, n_member))

    first, second = device(place - 2 + 4 * core), device(place + 2 - 4 * core)
    has_first = (even & has_down) | (odd & has_up)
    has_second = (even & has_up) | (odd & has_down)
    has_a, has_b, has_c = has_second, has_first, even | has_up
    gives_c = odd | has_up
    c_source = jnp.where(even, A, OWN)
    sibling = (slab, member + 1 - 2 * core)
    above, below = device(place + 1), device(place - 1)

    barrier = pltpu.get_barrier_semaphore()
    partners = ((has_first, first), (has_second, second), (place < count - 1, above), (place > 0, below))
    for there, other in partners:
        @pl.when(there)
        def _():
            pl.semaphore_signal(barrier, inc=1, device_id=other, device_id_type=MESH)

    def part(t):
        return pl.ds(pl.multiple_of(t * LANES, LANES), LANES)

    def group_at(g):
        return pl.ds(pl.multiple_of(g * GROUP, GROUP), GROUP)

    def order(slot, t, count):
        if slot == C:
            return t
        flip = core if slot == A else 1 - core
        return t + flip * (count - 1 - 2 * t)

    def load(t):
        return pltpu.make_async_copy(x_ref.at[part(t)], raw.at[part(t)], load_sem.at[t])

    def send(slot, t):
        source, target = {A: (OWN, first), B: (OWN, second), C: (c_source, sibling)}[slot]
        rows_of = part(order(slot, t, chunks))
        return pltpu.make_async_remote_copy(
            src_ref=blk.at[source, rows_of], dst_ref=blk.at[slot, rows_of],
            send_sem=send_sem.at[slot, t], recv_sem=recv_sem.at[slot, t],
            device_id=target, device_id_type=MESH)

    def send_tags(src_slot, dst_slot, target):
        return pltpu.make_async_remote_copy(
            src_ref=tags.at[src_slot], dst_ref=tags.at[dst_slot], send_sem=tag_send.at[dst_slot],
            recv_sem=tag_recv.at[dst_slot], device_id=target, device_id_type=MESH)

    load_ids = pltpu.make_async_copy(ids_ref, tags.at[OWN, 0:chunks], load_sem.at[chunks])
    load_keep = pltpu.make_async_copy(keep_ref, tags.at[OWN, chunks:2 * chunks], load_sem.at[chunks + 1])
    load(order(A, 0, chunks)).start()
    load_ids.start()
    load_keep.start()
    for t in range(1, chunks):
        load(order(A, t, chunks)).start()
    for slot, there in ((A, has_a), (B, has_b), (C, has_c)):
        @pl.when(jnp.logical_not(there))
        def _():
            tags[slot] = jnp.full(tags.shape[1:], -2, jnp.int32)
    pres[...] = jnp.full(pres.shape, OUT, jnp.float32)
    qacc[...] = jnp.full(qacc.shape, OUT, jnp.float32)

    def normalise(t):
        load(t).wait()
        values = raw[part(t), :].astype(jnp.float32)
        scale = lax.rsqrt(jnp.sum(values * values, axis=1, keepdims=True) + 1e-06)
        blk[OWN, part(t), :] = (values * scale).astype(jnp.bfloat16)

    normalise(order(A, 0, chunks))
    load_ids.wait()
    load_keep.wait()
    tags[OWN, chunks:2 * chunks] = jnp.where(tags[OWN, chunks:2 * chunks] == 1, tags[OWN, 0:chunks], -1)
    pl.semaphore_wait(barrier, sum(there.astype(jnp.int32) for there, _ in partners))

    @pl.when(has_first)
    def _():
        send(A, 0).start()
        send_tags(OWN, A, first).start()

    @pl.when(has_second)
    def _():
        send_tags(OWN, B, second).start()

    def prepare(t, _):
        normalise(order(A, t, chunks))

        @pl.when(has_first)
        def _():
            send(A, t).start()

        return 0

    lax.fori_loop(1, chunks, prepare, 0)

    @pl.when(odd)
    def _():
        for t in range(chunks):
            send(C, t).start()

    def row(slot, t):
        return tags[slot, pl.ds(t, 1), :]

    def columns(values):
        return jnp.broadcast_to(values, (LANES, LANES)).T

    def fold(values):
        return jnp.max(values.reshape(values.shape[0] // 8, 8, LANES), axis=0)

    def scores(p, q_slot, g):
        q = blk[q_slot, group_at(g), :]
        return lax.dot_general(p, q, (((1,), (1,)), ((), ())), preferred_element_type=jnp.float32)

    def own_step(t, _):
        p = blk[OWN, group_at(t), :]
        labels = jnp.concatenate(
            [columns(row(OWN, chunks + 2 * t + i).astype(jnp.float32)) for i in range(2)], axis=0)
        down = lax.broadcasted_iota(jnp.int32, (2 * LANES, LANES), 0) + t * 2 * LANES
        along = lax.broadcasted_iota(jnp.int32, (2 * LANES, LANES), 1)
        for n in range(chunks // 2):
            s = scores(p, OWN, n)
            for h in range(2):
                tile = 2 * n + h
                ids = row(OWN, tile).astype(jnp.float32)
                hits = (labels == ids) & (down != along + tile * LANES)
                top = fold(jnp.where(hits, s[:, h * LANES:(h + 1) * LANES], OUT))
                at = (0, slice(None), slice(tile * LANES, (tile + 1) * LANES))
                qacc[at] = jnp.maximum(qacc[at], top)
        return 0

    def shared(slot):
        low, high = tags[slot, 0:1, 0:1], tags[slot, chunks - 1:chunks, LANES - 1:LANES]
        if slot == C:
            return low
        return jnp.where(core == (0 if slot == A else 1), low, high)

    def biases(p_slot, t, size, cluster):
        each = [columns(jnp.where(row(p_slot, chunks + t + i) == cluster, 0.0, OUT)) for i in range(size)]
        return jnp.concatenate(each, axis=0) if size > 1 else each[0]

    def tile_pair(p, p_bias, best, q_slot, g, cluster, q_at):
        s = scores(p, q_slot, g)
        for h in range(2):
            one = s[:, h * LANES:(h + 1) * LANES]
            q_bias = jnp.where(row(q_slot, chunks + 2 * g + h) == cluster, 0.0, OUT)
            best = jnp.maximum(best, one + q_bias)
            at = (q_at, slice(None), part(2 * g + h))
            qacc[at] = jnp.maximum(qacc[at], fold(one + p_bias))
        return best

    def keep_rows(p_slot, t, size, best):
        for i in range(size):
            at = (p_slot - 1, slice(None), part(t + i))
            pres[at] = jnp.maximum(pres[at], fold(best[i * LANES:(i + 1) * LANES].T))

    def whole(p_slot, t, size, q_slot, cluster, q_at):
        p = blk[p_slot, pl.ds(pl.multiple_of(t * LANES, LANES), size * LANES), :]
        p_bias = biases(p_slot, t, size, cluster)
        best = jnp.full((size * LANES, LANES), OUT, jnp.float32)
        for g in range(groups):
            best = tile_pair(p, p_bias, best, q_slot, g, cluster, q_at)
        keep_rows(p_slot, t, size, best)

    def some(p_slot, g, q_slot, arrivals, cluster, q_at):
        p = blk[p_slot, group_at(g), :]
        p_bias = biases(p_slot, 2 * g, 2, cluster)
        best = jnp.full((GROUP, LANES), OUT, jnp.float32)
        for i in arrivals:
            best = tile_pair(p, p_bias, best, q_slot, order(q_slot, i, groups), cluster, q_at)
        keep_rows(p_slot, 2 * g, 2, best)

    lax.fori_loop(0, groups, own_step, 0)

    @pl.when(has_first)
    def _():
        for t in range(LEAD):
            send(A, t).wait_send()

    @pl.when(has_second)
    def _():
        for t in range(chunks):
            send(B, t).start()

    @pl.when(has_first)
    def _():
        send_tags(OWN, A, first).wait_send()

    @pl.when(has_second)
    def _():
        send_tags(OWN, B, second).wait_send()

    @pl.when(has_a)
    def _():
        send_tags(OWN, A, first).wait_recv()

    @pl.when(has_b)
    def _():
        send_tags(OWN, B, second).wait_recv()

    @pl.when(gives_c)
    def _():
        send_tags(c_source, C, sibling).start()
        send_tags(c_source, C, sibling).wait_send()

    @pl.when(has_c)
    def _():
        send_tags(c_source, C, sibling).wait_recv()

    s_a, s_b, s_c = shared(A), shared(B), shared(C)

    @pl.when(even)
    def _():
        for t in range(chunks):
            send(C, t).wait_recv()

    def step(j, _):
        @pl.when(has_a)
        def _():
            send(A, 2 * j).wait_recv()
            send(A, 2 * j + 1).wait_recv()

        @pl.when(even & has_a)
        def _():
            send(C, 2 * j).start()
            send(C, 2 * j + 1).start()

        @pl.when(has_a)
        def _():
            whole(A, 2 * order(A, j, groups), 2, OWN, s_a, 1)

        @pl.when(odd & has_c)
        def _():
            send(C, 2 * j).wait_recv()
            send(C, 2 * j + 1).wait_recv()

        @pl.when(has_c)
        def _():
            whole(C, 2 * j, 2, OWN, s_c, 2)

        for now in range(groups):
            @pl.when(odd & has_a & has_c & (j == now))
            def _():
                some(C, now, A, range(now + 1), s_c, 4)
                if now > 0:
                    some(A, order(A, now, groups), C, range(now), s_a, 5)

        m = j - 1

        @pl.when(has_b & (j > 0))
        def _():
            send(B, 2 * m).wait_recv()
            send(B, 2 * m + 1).wait_recv()

            @pl.when(even)
            def _():
                whole(B, 2 * order(B, m, groups), 2, C, s_b, 4)

            for now in range(groups - 1):
                @pl.when(has_a & (m == now))
                def _():
                    some(B, order(B, now, groups), A, range(min(now + 2, groups - now)), s_b, 3)

        return 0

    lax.fori_loop(0, groups, step, 0)

    def message(which, target):
        return pltpu.make_async_remote_copy(
            src_ref=msg.at[which], dst_ref=got.at[which], send_sem=msg_send.at[which],
            recv_sem=msg_recv.at[which], device_id=target, device_id_type=MESH)

    def masked(slot, tile, cluster, values):
        lanes = slice(tile * LANES, (tile + 1) * LANES)
        best = jnp.max(values[:, lanes], axis=0, keepdims=True)
        return jnp.where(row(slot, tile) == cluster, best, -1.0)

    @pl.when(odd & has_c)
    def _():
        for tile in range(chunks):
            msg[2, tile:tile + 1, :] = jnp.maximum(masked(C, tile, s_c, pres[2]), masked(C, tile, s_a, qacc[5]))
        message(2, above).start()

    @pl.when(has_a & has_b)
    def _():
        some(B, order(B, 0, groups), A, range(2, groups), s_b, 3)

    def last_step(t, _):
        @pl.when(has_b)
        def _():
            send(B, t).wait_recv()

        @pl.when(even & has_b)
        def _():
            whole(B, order(B, t, chunks), 1, C, s_b, 4)

        return 0

    lax.fori_loop(chunks - 2, chunks, last_step, 0)

    @pl.when(has_a & has_b)
    def _():
        some(B, order(B, groups - 1, groups), A, range(1), s_b, 3)

    for tile in range(chunks):
        msg[0, tile:tile + 1, :] = jnp.maximum(
            jnp.maximum(masked(A, tile, s_a, pres[0]), masked(A, tile, s_b, qacc[3])),
            jnp.where(odd, masked(A, tile, s_c, qacc[4]), -1.0))
        msg[1, tile:tile + 1, :] = masked(B, tile, s_b, pres[1])

    @pl.when(has_a)
    def _():
        message(0, second).start()

    @pl.when(has_b)
    def _():
        message(1, first).start()

    @pl.when(even)
    def _():
        for tile in range(chunks):
            msg[2, tile:tile + 1, :] = jnp.maximum(masked(C, tile, s_c, pres[2]), masked(C, tile, s_b, qacc[4]))
        message(2, above).start()

    messages = ((has_a, second, has_first), (has_b, first, has_second), (has_c, above, odd | has_down))
    for tile in range(chunks):
        lanes = slice(tile * LANES, (tile + 1) * LANES)
        own = jnp.max(qacc[0, :, lanes], axis=0, keepdims=True)
        out_ref[tile:tile + 1, :] = jnp.maximum(
            jnp.maximum(own, -1.0),
            jnp.maximum(masked(OWN, tile, s_a, qacc[1]), masked(OWN, tile, s_c, qacc[2])))

    @pl.when(has_first)
    def _():
        for t in range(LEAD, chunks):
            send(A, t).wait_send()

    @pl.when(has_second)
    def _():
        for t in range(chunks):
            send(B, t).wait_send()

    @pl.when(gives_c)
    def _():
        for t in range(chunks):
            send(C, t).wait_send()

    for which, (gives, target, gets) in enumerate(messages):
        @pl.when(gives)
        def _():
            message(which, target).wait_send()

        @pl.when(gets)
        def _():
            message(which, target).wait_recv()
            out_ref[...] = jnp.maximum(out_ref[...], got[which])


def shards(n_slab, n_member, embeddings, cluster_ids, keep_mask):
    rows, width = embeddings.shape
    chunks = rows // LANES
    highest = pl.pallas_call(
        functools.partial(kernel, n_slab, n_member),
        out_shape=jax.ShapeDtypeStruct((chunks, LANES), jnp.float32),
        in_specs=[pl.BlockSpec(memory_space=pltpu.HBM)] * 3,
        out_specs=pl.BlockSpec(memory_space=pltpu.VMEM),
        scratch_shapes=[
            pltpu.VMEM((rows, width), jnp.bfloat16),
            pltpu.VMEM((4, rows, width), jnp.bfloat16),
            pltpu.VMEM((4, 2 * chunks, LANES), jnp.int32),
            pltpu.VMEM((3, 8, rows), jnp.float32),
            pltpu.VMEM((6, 8, rows), jnp.float32),
            pltpu.VMEM((3, chunks, LANES), jnp.float32),
            pltpu.VMEM((3, chunks, LANES), jnp.float32),
            pltpu.SemaphoreType.DMA((chunks + 2,)),
            pltpu.SemaphoreType.DMA((4, chunks)),
            pltpu.SemaphoreType.DMA((4, chunks)),
            pltpu.SemaphoreType.DMA((4,)),
            pltpu.SemaphoreType.DMA((4,)),
            pltpu.SemaphoreType.DMA((3,)),
            pltpu.SemaphoreType.DMA((3,)),
        ],
        compiler_params=pltpu.CompilerParams(
            collective_id=0, has_side_effects=True, vmem_limit_bytes=40 << 20),
    )(*(pltpu.with_memory_space_constraint(each, pltpu.HBM) for each in (
        embeddings, cluster_ids.reshape(chunks, LANES), keep_mask.reshape(chunks, LANES))))
    return highest.reshape(rows)


def solution(mesh):
    placed = (P(("slab", "member"), None), P(("slab", "member")), P(("slab", "member")))
    return jax.shard_map(
        functools.partial(shards, mesh.shape["slab"], mesh.shape["member"]),
        mesh=mesh, in_specs=placed, out_specs=P(("slab", "member")), check_vma=False,
    )
```

```python
import functools

import jax
import jax.numpy as jnp
from jax import lax
from jax.experimental import pallas as pl
from jax.experimental.pallas import tpu as pltpu
from jax.sharding import PartitionSpec as P

MESH = pl.DeviceIdType.MESH
OWN, A, B, C = 0, 1, 2, 3
LANES = 128
GROUP = 2 * LANES
LEAD = 4
PLANE = 16
OVER = 2
OUT = -4.0


def kernel(n_slab, n_member, x_ref, ids_ref, keep_ref, out_ref, raw, blk, tags, pres, qacc, msg, got,
           relay, load_sem, send_sem, recv_sem, tag_send, tag_recv, msg_send, msg_recv, over_send, over_recv, ready):
    rows, width = raw.shape
    chunks, groups = rows // LANES, rows // GROUP
    count = n_slab * n_member
    slab, member = lax.axis_index("slab"), lax.axis_index("member")
    core = lax.rem(member, 2)
    place = slab * n_member + member
    chip = lax.div(place, 2)
    has_down, has_up = chip > 0, chip < count // 2 - 1
    even, odd = core == 0, core == 1

    def device(at):
        at = jnp.clip(at, 0, count - 1)
        return (lax.div(at, n_member), lax.rem(at, n_member))

    first, second = device(place - 2 + 4 * core), device(place + 2 - 4 * core)
    has_first = (even & has_down) | (odd & has_up)
    has_second = (even & has_up) | (odd & has_down)
    has_a, has_b, has_c = has_second, has_first, even | has_up
    gives_c = odd | has_up
    step_at = lax.rem(chip, PLANE)
    over_r, over_l = odd & (step_at == 0) & has_down, odd & (step_at == PLANE - 1) & has_up
    over_y = odd & (chip == count // 2 - 1)
    crossings = count // 2 // PLANE - 1
    crossing = lax.div(chip + 1, PLANE) - 1
    over_first, over_next = over_r & (crossing == 0), over_r & (crossing == 1)
    over_to_y = over_r & jnp.logical_not(over_first)
    c_source = jnp.where(even, A, OWN)
    sibling = (slab, member + 1 - 2 * core)
    above, below = device(place + 1), device(place - 1)

    barrier = pltpu.get_barrier_semaphore()
    partners = ((has_first, first), (has_second, second), (place < count - 1, above), (place > 0, below))
    told = partners + ((over_to_y | over_l, device(count - 1)), (over_next, device(place - 2 * PLANE)))
    for there, other in told:
        @pl.when(there)
        def _():
            pl.semaphore_signal(barrier, inc=1, device_id=other, device_id_type=MESH)

    def part(t):
        return pl.ds(pl.multiple_of(t * LANES, LANES), LANES)

    def group_at(g):
        return pl.ds(pl.multiple_of(g * GROUP, GROUP), GROUP)

    def order(slot, t, count):
        if slot == C:
            return t
        flip = core if slot == A else 1 - core
        return t + flip * (count - 1 - 2 * t)

    def load(t):
        return pltpu.make_async_copy(x_ref.at[part(t)], raw.at[part(t)], load_sem.at[t])

    def send(slot, t):
        source, target = {A: (OWN, first), B: (OWN, second), C: (c_source, sibling)}[slot]
        rows_of = part(order(slot, t, chunks))
        return pltpu.make_async_remote_copy(
            src_ref=blk.at[source, rows_of], dst_ref=blk.at[slot, rows_of],
            send_sem=send_sem.at[slot, t], recv_sem=recv_sem.at[slot, t],
            device_id=target, device_id_type=MESH)

    def send_tags(src_slot, dst_slot, target):
        return pltpu.make_async_remote_copy(
            src_ref=tags.at[src_slot], dst_ref=tags.at[dst_slot], send_sem=tag_send.at[dst_slot],
            recv_sem=tag_recv.at[dst_slot], device_id=target, device_id_type=MESH)

    load_ids = pltpu.make_async_copy(ids_ref, tags.at[OWN, 0:chunks], load_sem.at[chunks])
    load_keep = pltpu.make_async_copy(keep_ref, tags.at[OWN, chunks:2 * chunks], load_sem.at[chunks + 1])
    load(order(A, 0, chunks)).start()
    load_ids.start()
    load_keep.start()
    for t in range(1, chunks):
        load(order(A, t, chunks)).start()
    for slot, there in ((A, has_a), (B, has_b), (C, has_c)):
        @pl.when(jnp.logical_not(there))
        def _():
            tags[slot] = jnp.full(tags.shape[1:], -2, jnp.int32)
    pres[...] = jnp.full(pres.shape, OUT, jnp.float32)
    qacc[...] = jnp.full(qacc.shape, OUT, jnp.float32)

    def normalise(t):
        load(t).wait()
        values = raw[part(t), :].astype(jnp.float32)
        scale = lax.rsqrt(jnp.sum(values * values, axis=1, keepdims=True) + 1e-06)
        blk[OWN, part(t), :] = (values * scale).astype(jnp.bfloat16)

    normalise(order(A, 0, chunks))
    load_ids.wait()
    load_keep.wait()
    tags[OWN, chunks:2 * chunks] = jnp.where(tags[OWN, chunks:2 * chunks] == 1, tags[OWN, 0:chunks], -1)
    heard = sum(there.astype(jnp.int32) for there, _ in partners)
    heard = heard + over_first.astype(jnp.int32) + over_y.astype(jnp.int32) * (2 * crossings - 1)
    pl.semaphore_wait(barrier, heard)

    @pl.when(over_y)
    def _():
        for i in range(1, crossings):
            pl.semaphore_signal(ready, inc=1, device_id=device(2 * PLANE * (i + 1) + 1), device_id_type=MESH)

    @pl.when(has_first)
    def _():
        send(A, 0).start()
        send_tags(OWN, A, first).start()

    @pl.when(has_second)
    def _():
        send_tags(OWN, B, second).start()

    def prepare(t, _):
        normalise(order(A, t, chunks))

        @pl.when(has_first)
        def _():
            send(A, t).start()

        return 0

    lax.fori_loop(1, chunks, prepare, 0)

    @pl.when(odd)
    def _():
        for t in range(chunks):
            send(C, t).start()

    def row(slot, t):
        return tags[slot, pl.ds(t, 1), :]

    def columns(values):
        return jnp.broadcast_to(values, (LANES, LANES)).T

    def fold(values):
        return jnp.max(values.reshape(values.shape[0] // 8, 8, LANES), axis=0)

    def scores(p, q_slot, g):
        q = blk[q_slot, group_at(g), :]
        return lax.dot_general(p, q, (((1,), (1,)), ((), ())), preferred_element_type=jnp.float32)

    def own_step(t, _):
        p = blk[OWN, group_at(t), :]
        labels = jnp.concatenate(
            [columns(row(OWN, chunks + 2 * t + i).astype(jnp.float32)) for i in range(2)], axis=0)
        down = lax.broadcasted_iota(jnp.int32, (2 * LANES, LANES), 0) + t * 2 * LANES
        along = lax.broadcasted_iota(jnp.int32, (2 * LANES, LANES), 1)
        for n in range(chunks // 2):
            s = scores(p, OWN, n)
            for h in range(2):
                tile = 2 * n + h
                ids = row(OWN, tile).astype(jnp.float32)
                hits = (labels == ids) & (down != along + tile * LANES)
                top = fold(jnp.where(hits, s[:, h * LANES:(h + 1) * LANES], OUT))
                at = (0, slice(None), slice(tile * LANES, (tile + 1) * LANES))
                qacc[at] = jnp.maximum(qacc[at], top)
        return 0

    def shared(slot):
        low, high = tags[slot, 0:1, 0:1], tags[slot, chunks - 1:chunks, LANES - 1:LANES]
        if slot == C:
            return low
        return jnp.where(core == (0 if slot == A else 1), low, high)

    def biases(p_slot, t, size, cluster):
        each = [columns(jnp.where(row(p_slot, chunks + t + i) == cluster, 0.0, OUT)) for i in range(size)]
        return jnp.concatenate(each, axis=0) if size > 1 else each[0]

    def tile_pair(p, p_bias, best, q_slot, g, cluster, q_at):
        s = scores(p, q_slot, g)
        for h in range(2):
            one = s[:, h * LANES:(h + 1) * LANES]
            q_bias = jnp.where(row(q_slot, chunks + 2 * g + h) == cluster, 0.0, OUT)
            best = jnp.maximum(best, one + q_bias)
            at = (q_at, slice(None), part(2 * g + h))
            qacc[at] = jnp.maximum(qacc[at], fold(one + p_bias))
        return best

    def keep_rows(p_slot, t, size, best):
        for i in range(size):
            at = (p_slot - 1, slice(None), part(t + i))
            pres[at] = jnp.maximum(pres[at], fold(best[i * LANES:(i + 1) * LANES].T))

    def whole(p_slot, t, size, q_slot, cluster, q_at):
        p = blk[p_slot, pl.ds(pl.multiple_of(t * LANES, LANES), size * LANES), :]
        p_bias = biases(p_slot, t, size, cluster)
        best = jnp.full((size * LANES, LANES), OUT, jnp.float32)
        for g in range(groups):
            best = tile_pair(p, p_bias, best, q_slot, g, cluster, q_at)
        keep_rows(p_slot, t, size, best)

    def some(p_slot, t, size, q_slot, arrivals, cluster, q_at):
        p = blk[p_slot, pl.ds(pl.multiple_of(t * LANES, LANES), size * LANES), :]
        p_bias = biases(p_slot, t, size, cluster)
        best = jnp.full((size * LANES, LANES), OUT, jnp.float32)
        for i in arrivals:
            best = tile_pair(p, p_bias, best, q_slot, order(q_slot, i, groups), cluster, q_at)
        keep_rows(p_slot, t, size, best)

    lax.fori_loop(0, groups, own_step, 0)

    over_target = device(jnp.where(crossing == 0, place + 2 * PLANE, count - 1))

    def over_l_at(i):
        return device(2 * (PLANE * (i + 1) - 1) + 1)

    def over(i, t, way, target):
        source, there = way
        rows_of = part(chunks - OVER + t)
        return pltpu.make_async_remote_copy(
            src_ref=relay.at[i, t] if source is relay else blk.at[OWN, rows_of],
            dst_ref=relay.at[i, t] if there is relay else blk.at[B, rows_of],
            send_sem=over_send.at[i, t], recv_sem=over_recv.at[i, t] if there is relay else recv_sem.at[B, chunks - OVER + t],
            device_id=target, device_id_type=MESH)

    @pl.when(over_to_y)
    def _():
        pl.semaphore_wait(ready, 1)

    @pl.when(over_r)
    def _():
        for t in range(OVER):
            over(crossing, t, (OWN, relay), over_target).start()

    @pl.when(has_first)
    def _():
        for t in range(LEAD):
            send(A, t).wait_send()

    @pl.when(has_second)
    def _():
        for t in range(chunks - OVER):
            send(B, t).start()

    @pl.when(has_second & jnp.logical_not(over_r))
    def _():
        for t in range(chunks - OVER, chunks):
            send(B, t).start()

    @pl.when(over_next)
    def _():
        for t in range(OVER):
            over(0, t, (OWN, relay), first).wait_recv()
            over(0, t, (relay, relay), over_target).start()

    @pl.when(has_first)
    def _():
        send_tags(OWN, A, first).wait_send()

    @pl.when(has_second)
    def _():
        send_tags(OWN, B, second).wait_send()

    @pl.when(has_a)
    def _():
        send_tags(OWN, A, first).wait_recv()

    @pl.when(has_b)
    def _():
        send_tags(OWN, B, second).wait_recv()

    @pl.when(gives_c)
    def _():
        send_tags(c_source, C, sibling).start()
        send_tags(c_source, C, sibling).wait_send()

    @pl.when(has_c)
    def _():
        send_tags(c_source, C, sibling).wait_recv()

    s_a, s_b, s_c = shared(A), shared(B), shared(C)

    @pl.when(even)
    def _():
        for t in range(chunks):
            send(C, t).wait_recv()

    def step(j, _):
        @pl.when(over_y & (j == groups - 1))
        def _():
            for i in range(crossings):
                for t in range(OVER):
                    over(i, t, (OWN, relay), first).wait_recv()
                    over(i, t, (relay, B), over_l_at(i)).start()

        @pl.when(has_a)
        def _():
            send(A, 2 * j).wait_recv()
            send(A, 2 * j + 1).wait_recv()

        @pl.when(even & has_a)
        def _():
            send(C, 2 * j).start()
            send(C, 2 * j + 1).start()

        @pl.when(has_a)
        def _():
            whole(A, 2 * order(A, j, groups), 2, OWN, s_a, 1)

        @pl.when(odd & has_c)
        def _():
            send(C, 2 * j).wait_recv()
            send(C, 2 * j + 1).wait_recv()

        @pl.when(has_c)
        def _():
            whole(C, 2 * j, 2, OWN, s_c, 2)

        for now in range(groups):
            @pl.when(odd & has_a & has_c & (j == now))
            def _():
                some(C, 2 * now, 2, A, range(now + 1), s_c, 4)
                if now > 0:
                    some(A, 2 * order(A, now, groups), 2, C, range(now), s_a, 5)

        m = j - 1

        @pl.when(has_b & (j > 0))
        def _():
            send(B, 2 * m).wait_recv()
            send(B, 2 * m + 1).wait_recv()

            @pl.when(even)
            def _():
                whole(B, 2 * order(B, m, groups), 2, C, s_b, 4)

            for now in range(groups - 1):
                @pl.when(has_a & (m == now))
                def _():
                    some(B, 2 * order(B, now, groups), 2, A, range(min(now + 2, groups - now)), s_b, 3)

        return 0

    lax.fori_loop(0, groups, step, 0)

    def message(which, target):
        return pltpu.make_async_remote_copy(
            src_ref=msg.at[which], dst_ref=got.at[which], send_sem=msg_send.at[which],
            recv_sem=msg_recv.at[which], device_id=target, device_id_type=MESH)

    def masked(slot, tile, cluster, values):
        return jnp.where(row(slot, tile) == cluster, jnp.max(values, axis=0, keepdims=True), -1.0)

    def message_a(tile):
        msg[0, pl.ds(tile, 1), :] = jnp.maximum(
            jnp.maximum(masked(A, tile, s_a, pres[0, :, part(tile)]), masked(A, tile, s_b, qacc[3, :, part(tile)])),
            jnp.where(odd, masked(A, tile, s_c, qacc[4, :, part(tile)]), -1.0))

    def message_b(tile):
        msg[1, pl.ds(tile, 1), :] = masked(B, tile, s_b, pres[1, :, part(tile)])

    for tile in range(chunks):
        msg[2, tile:tile + 1, :] = jnp.maximum(
            masked(C, tile, s_c, pres[2, :, part(tile)]), jnp.where(odd, masked(C, tile, s_a, qacc[5, :, part(tile)]), -1.0))

    @pl.when(odd & has_c)
    def _():
        message(2, above).start()

    for tile in range(chunks):
        own = jnp.max(qacc[0, :, part(tile)], axis=0, keepdims=True)
        out_ref[tile:tile + 1, :] = jnp.maximum(
            jnp.maximum(own, -1.0),
            jnp.maximum(masked(OWN, tile, s_a, qacc[1, :, part(tile)]), masked(OWN, tile, s_c, qacc[2, :, part(tile)])))

    @pl.when(has_a & has_b)
    def _():
        some(B, 2 * order(B, 0, groups), 2, A, range(2, groups), s_b, 3)

    for t in range(2, chunks):
        message_a(order(A, t, chunks))
    for t in range(chunks - 2):
        message_b(order(B, t, chunks))

    def last_step(t, _):
        @pl.when(has_b)
        def _():
            send(B, t).wait_recv()

        @pl.when(has_a & has_b)
        def _():
            some(B, order(B, t, chunks), 1, A, range(1), s_b, 3)

        @pl.when(t == chunks - 1)
        def _():
            for i in range(2):
                message_a(order(A, i, chunks))

            @pl.when(has_a)
            def _():
                message(0, second).start()

        @pl.when(even & has_b)
        def _():
            whole(B, order(B, t, chunks), 1, C, s_b, 4)

        @pl.when(has_b)
        def _():
            message_b(order(B, t, chunks))

        return 0

    lax.fori_loop(chunks - 2, chunks, last_step, 0)

    @pl.when(has_b)
    def _():
        message(1, first).start()

    @pl.when(even)
    def _():
        for tile in range(chunks):
            msg[2, tile:tile + 1, :] = jnp.maximum(
                msg[2, tile:tile + 1, :], masked(C, tile, s_b, qacc[4, :, part(tile)]))
        message(2, above).start()

    messages = ((has_a, second, has_first), (has_b, first, has_second), (has_c, above, odd | has_down))
    @pl.when(has_first)
    def _():
        for t in range(LEAD, chunks):
            send(A, t).wait_send()

    @pl.when(has_second)
    def _():
        for t in range(chunks - OVER):
            send(B, t).wait_send()

    @pl.when(has_second & jnp.logical_not(over_r))
    def _():
        for t in range(chunks - OVER, chunks):
            send(B, t).wait_send()

    @pl.when(over_r)
    def _():
        for t in range(OVER):
            over(crossing, t, (OWN, relay), over_target).wait_send()

    @pl.when(over_next)
    def _():
        for t in range(OVER):
            over(0, t, (relay, relay), over_target).wait_send()

    @pl.when(over_y)
    def _():
        for i in range(crossings):
            for t in range(OVER):
                over(i, t, (relay, B), over_l_at(i)).wait_send()

    @pl.when(gives_c)
    def _():
        for t in range(chunks):
            send(C, t).wait_send()

    for which, (gives, target, gets) in enumerate(messages):
        @pl.when(gives)
        def _():
            message(which, target).wait_send()

        @pl.when(gets)
        def _():
            message(which, target).wait_recv()
            out_ref[...] = jnp.maximum(out_ref[...], got[which])


def shards(n_slab, n_member, embeddings, cluster_ids, keep_mask):
    rows, width = embeddings.shape
    chunks = rows // LANES
    crossings = n_slab * n_member // 2 // PLANE - 1
    highest = pl.pallas_call(
        functools.partial(kernel, n_slab, n_member),
        out_shape=jax.ShapeDtypeStruct((chunks, LANES), jnp.float32),
        in_specs=[pl.BlockSpec(memory_space=pltpu.HBM)] * 3,
        out_specs=pl.BlockSpec(memory_space=pltpu.VMEM),
        scratch_shapes=[
            pltpu.VMEM((rows, width), jnp.bfloat16),
            pltpu.VMEM((4, rows, width), jnp.bfloat16),
            pltpu.VMEM((4, 2 * chunks, LANES), jnp.int32),
            pltpu.VMEM((3, 8, rows), jnp.float32),
            pltpu.VMEM((6, 8, rows), jnp.float32),
            pltpu.VMEM((3, chunks, LANES), jnp.float32),
            pltpu.VMEM((3, chunks, LANES), jnp.float32),
            pltpu.VMEM((crossings, OVER, LANES, width), jnp.bfloat16),
            pltpu.SemaphoreType.DMA((chunks + 2,)),
            pltpu.SemaphoreType.DMA((4, chunks)),
            pltpu.SemaphoreType.DMA((4, chunks)),
            pltpu.SemaphoreType.DMA((4,)),
            pltpu.SemaphoreType.DMA((4,)),
            pltpu.SemaphoreType.DMA((3,)),
            pltpu.SemaphoreType.DMA((3,)),
            pltpu.SemaphoreType.DMA((crossings, OVER)),
            pltpu.SemaphoreType.DMA((crossings, OVER)),
            pltpu.SemaphoreType.REGULAR,
        ],
        compiler_params=pltpu.CompilerParams(
            collective_id=0, has_side_effects=True, vmem_limit_bytes=40 << 20),
    )(*(pltpu.with_memory_space_constraint(each, pltpu.HBM) for each in (
        embeddings, cluster_ids.reshape(chunks, LANES), keep_mask.reshape(chunks, LANES))))
    return highest.reshape(rows)


def solution(mesh):
    placed = (P(("slab", "member"), None), P(("slab", "member")), P(("slab", "member")))
    return jax.shard_map(
        functools.partial(shards, mesh.shape["slab"], mesh.shape["member"]),
        mesh=mesh, in_specs=placed, out_specs=P(("slab", "member")), check_vma=False,
    )
```

```python
import functools

import jax
import jax.numpy as jnp
from jax import lax
from jax.experimental import pallas as pl
from jax.experimental.pallas import tpu as pltpu
from jax.sharding import PartitionSpec as P

MESH = pl.DeviceIdType.MESH
OWN, A, B, C = 0, 1, 2, 3
LANES = 128
GROUP = 2 * LANES
LEAD = 5
PLANE = 16
OVER = 3
OUT = -4.0


def kernel(n_slab, n_member, x_ref, ids_ref, keep_ref, out_ref, raw, blk, tags, pres, qacc, msg, got,
           relay, load_sem, send_sem, recv_sem, tag_send, tag_recv, msg_send, msg_recv, over_send, over_recv, ready):
    rows, width = raw.shape
    chunks, groups = rows // LANES, rows // GROUP
    count = n_slab * n_member
    slab, member = lax.axis_index("slab"), lax.axis_index("member")
    core = lax.rem(member, 2)
    place = slab * n_member + member
    chip = lax.div(place, 2)
    has_down, has_up = chip > 0, chip < count // 2 - 1
    even, odd = core == 0, core == 1

    def device(at):
        at = jnp.clip(at, 0, count - 1)
        return (lax.div(at, n_member), lax.rem(at, n_member))

    first, second = device(place - 2 + 4 * core), device(place + 2 - 4 * core)
    has_first = (even & has_down) | (odd & has_up)
    has_second = (even & has_up) | (odd & has_down)
    has_a, has_b, has_c = has_second, has_first, even | has_up
    gives_c = odd | has_up
    step_at = lax.rem(chip, PLANE)
    over_r, over_l = odd & (step_at == 0) & has_down, odd & (step_at == PLANE - 1) & has_up
    over_y = odd & (chip == count // 2 - 1)
    crossings = count // 2 // PLANE - 1
    crossing = lax.div(chip + 1, PLANE) - 1
    over_first, over_next = over_r & (crossing == 0), over_r & (crossing == 1)
    over_to_y = over_r & jnp.logical_not(over_first)
    c_source = jnp.where(even, A, OWN)
    sibling = (slab, member + 1 - 2 * core)
    above, below = device(place + 1), device(place - 1)

    barrier = pltpu.get_barrier_semaphore()
    partners = ((has_first, first), (has_second, second), (place < count - 1, above), (place > 0, below))
    told = partners + ((over_to_y | over_l, device(count - 1)), (over_next, device(place - 2 * PLANE)))
    for there, other in told:
        @pl.when(there)
        def _():
            pl.semaphore_signal(barrier, inc=1, device_id=other, device_id_type=MESH)

    def part(t):
        return pl.ds(pl.multiple_of(t * LANES, LANES), LANES)

    def group_at(g):
        return pl.ds(pl.multiple_of(g * GROUP, GROUP), GROUP)

    def order(slot, t, count):
        if slot == C:
            return t
        flip = core if slot == A else 1 - core
        return t + flip * (count - 1 - 2 * t)

    def load(t):
        return pltpu.make_async_copy(x_ref.at[part(t)], raw.at[part(t)], load_sem.at[t])

    def send(slot, t):
        source, target = {A: (OWN, first), B: (OWN, second), C: (c_source, sibling)}[slot]
        rows_of = part(order(slot, t, chunks))
        return pltpu.make_async_remote_copy(
            src_ref=blk.at[source, rows_of], dst_ref=blk.at[slot, rows_of],
            send_sem=send_sem.at[slot, t], recv_sem=recv_sem.at[slot, t],
            device_id=target, device_id_type=MESH)

    def send_tags(src_slot, dst_slot, target):
        return pltpu.make_async_remote_copy(
            src_ref=tags.at[src_slot], dst_ref=tags.at[dst_slot], send_sem=tag_send.at[dst_slot],
            recv_sem=tag_recv.at[dst_slot], device_id=target, device_id_type=MESH)

    load_ids = pltpu.make_async_copy(ids_ref, tags.at[OWN, 0:chunks], load_sem.at[chunks])
    load_keep = pltpu.make_async_copy(keep_ref, tags.at[OWN, chunks:2 * chunks], load_sem.at[chunks + 1])
    load(order(A, 0, chunks)).start()
    load_ids.start()
    load_keep.start()
    for t in range(1, chunks):
        load(order(A, t, chunks)).start()
    for slot, there in ((A, has_a), (B, has_b), (C, has_c)):
        @pl.when(jnp.logical_not(there))
        def _():
            tags[slot] = jnp.full(tags.shape[1:], -2, jnp.int32)
    pres[...] = jnp.full(pres.shape, OUT, jnp.float32)
    qacc[...] = jnp.full(qacc.shape, OUT, jnp.float32)

    def normalise(t):
        load(t).wait()
        values = raw[part(t), :].astype(jnp.float32)
        scale = lax.rsqrt(jnp.sum(values * values, axis=1, keepdims=True) + 1e-06)
        blk[OWN, part(t), :] = (values * scale).astype(jnp.bfloat16)

    normalise(order(A, 0, chunks))
    load_ids.wait()
    load_keep.wait()
    tags[OWN, chunks:2 * chunks] = jnp.where(tags[OWN, chunks:2 * chunks] == 1, tags[OWN, 0:chunks], -1)
    heard = sum(there.astype(jnp.int32) for there, _ in partners)
    heard = heard + over_first.astype(jnp.int32) + over_y.astype(jnp.int32) * (2 * crossings - 1)
    pl.semaphore_wait(barrier, heard)

    @pl.when(over_y)
    def _():
        for i in range(1, crossings):
            pl.semaphore_signal(ready, inc=1, device_id=device(2 * PLANE * (i + 1) + 1), device_id_type=MESH)

    @pl.when(has_first)
    def _():
        send(A, 0).start()
        send_tags(OWN, A, first).start()

    @pl.when(has_second)
    def _():
        send_tags(OWN, B, second).start()

    def prepare(t, _):
        normalise(order(A, t, chunks))

        @pl.when(has_first)
        def _():
            send(A, t).start()

        return 0

    lax.fori_loop(1, chunks, prepare, 0)

    @pl.when(odd)
    def _():
        for t in range(chunks):
            send(C, t).start()

    def row(slot, t):
        return tags[slot, pl.ds(t, 1), :]

    def columns(values):
        return jnp.broadcast_to(values, (LANES, LANES)).T

    def fold(values):
        return jnp.max(values.reshape(values.shape[0] // 8, 8, LANES), axis=0)

    def scores(p, q_slot, g):
        q = blk[q_slot, group_at(g), :]
        return lax.dot_general(p, q, (((1,), (1,)), ((), ())), preferred_element_type=jnp.float32)

    def own_step(t, _):
        p = blk[OWN, group_at(t), :]
        labels = jnp.concatenate(
            [columns(row(OWN, chunks + 2 * t + i).astype(jnp.float32)) for i in range(2)], axis=0)
        down = lax.broadcasted_iota(jnp.int32, (2 * LANES, LANES), 0) + t * 2 * LANES
        along = lax.broadcasted_iota(jnp.int32, (2 * LANES, LANES), 1)
        for n in range(chunks // 2):
            s = scores(p, OWN, n)
            for h in range(2):
                tile = 2 * n + h
                ids = row(OWN, tile).astype(jnp.float32)
                hits = (labels == ids) & (down != along + tile * LANES)
                top = fold(jnp.where(hits, s[:, h * LANES:(h + 1) * LANES], OUT))
                at = (0, slice(None), slice(tile * LANES, (tile + 1) * LANES))
                qacc[at] = jnp.maximum(qacc[at], top)
        return 0

    def shared(slot):
        low, high = tags[slot, 0:1, 0:1], tags[slot, chunks - 1:chunks, LANES - 1:LANES]
        if slot == C:
            return low
        return jnp.where(core == (0 if slot == A else 1), low, high)

    def biases(p_slot, t, size, cluster):
        each = [columns(jnp.where(row(p_slot, chunks + t + i) == cluster, 0.0, OUT)) for i in range(size)]
        return jnp.concatenate(each, axis=0) if size > 1 else each[0]

    def tile_pair(p, p_bias, best, q_slot, g, cluster, q_at):
        s = scores(p, q_slot, g)
        for h in range(2):
            one = s[:, h * LANES:(h + 1) * LANES]
            q_bias = jnp.where(row(q_slot, chunks + 2 * g + h) == cluster, 0.0, OUT)
            best = jnp.maximum(best, one + q_bias)
            at = (q_at, slice(None), part(2 * g + h))
            qacc[at] = jnp.maximum(qacc[at], fold(one + p_bias))
        return best

    def keep_rows(p_slot, t, size, best):
        for i in range(size):
            at = (p_slot - 1, slice(None), part(t + i))
            pres[at] = jnp.maximum(pres[at], fold(best[i * LANES:(i + 1) * LANES].T))

    def whole(p_slot, t, size, q_slot, cluster, q_at):
        p = blk[p_slot, pl.ds(pl.multiple_of(t * LANES, LANES), size * LANES), :]
        p_bias = biases(p_slot, t, size, cluster)
        best = jnp.full((size * LANES, LANES), OUT, jnp.float32)
        for g in range(groups):
            best = tile_pair(p, p_bias, best, q_slot, g, cluster, q_at)
        keep_rows(p_slot, t, size, best)

    def some(p_slot, t, size, q_slot, arrivals, cluster, q_at):
        p = blk[p_slot, pl.ds(pl.multiple_of(t * LANES, LANES), size * LANES), :]
        p_bias = biases(p_slot, t, size, cluster)
        best = jnp.full((size * LANES, LANES), OUT, jnp.float32)
        for i in arrivals:
            best = tile_pair(p, p_bias, best, q_slot, order(q_slot, i, groups), cluster, q_at)
        keep_rows(p_slot, t, size, best)

    over_target = device(jnp.where(crossing == 0, place + 2 * PLANE, count - 1))

    def over_l_at(i):
        return device(2 * (PLANE * (i + 1) - 1) + 1)

    def over(i, t, way, target):
        source, there = way
        rows_of = part(chunks - OVER + t)
        return pltpu.make_async_remote_copy(
            src_ref=relay.at[i, t] if source is relay else blk.at[OWN, rows_of],
            dst_ref=relay.at[i, t] if there is relay else blk.at[B, rows_of],
            send_sem=over_send.at[i, t], recv_sem=over_recv.at[i, t] if there is relay else recv_sem.at[B, chunks - OVER + t],
            device_id=target, device_id_type=MESH)

    @pl.when(over_first)
    def _():
        for t in range(OVER):
            over(crossing, t, (OWN, relay), over_target).start()

    lax.fori_loop(0, groups, own_step, 0)

    @pl.when(over_to_y)
    def _():
        pl.semaphore_wait(ready, 1)
        for t in range(OVER):
            over(crossing, t, (OWN, relay), over_target).start()

    @pl.when(over_next)
    def _():
        for t in range(OVER):
            over(0, t, (OWN, relay), first).wait_recv()
            over(0, t, (relay, relay), over_target).start()

    @pl.when(has_first)
    def _():
        for t in range(LEAD):
            send(A, t).wait_send()

    @pl.when(has_second)
    def _():
        for t in range(chunks - OVER):
            send(B, t).start()

    @pl.when(has_second & jnp.logical_not(over_r))
    def _():
        for t in range(chunks - OVER, chunks):
            send(B, t).start()

    @pl.when(has_first)
    def _():
        send_tags(OWN, A, first).wait_send()

    @pl.when(has_second)
    def _():
        send_tags(OWN, B, second).wait_send()

    @pl.when(has_a)
    def _():
        send_tags(OWN, A, first).wait_recv()

    @pl.when(has_b)
    def _():
        send_tags(OWN, B, second).wait_recv()

    @pl.when(gives_c)
    def _():
        send_tags(c_source, C, sibling).start()
        send_tags(c_source, C, sibling).wait_send()

    @pl.when(has_c)
    def _():
        send_tags(c_source, C, sibling).wait_recv()

    s_a, s_b, s_c = shared(A), shared(B), shared(C)

    @pl.when(even)
    def _():
        for t in range(chunks):
            send(C, t).wait_recv()

    def step(j, _):
        @pl.when(over_y & (j == groups - 2))
        def _():
            for i in range(crossings):
                for t in range(OVER):
                    over(i, t, (OWN, relay), first).wait_recv()
                    over(i, t, (relay, B), over_l_at(i)).start()

        @pl.when(has_a)
        def _():
            send(A, 2 * j).wait_recv()
            send(A, 2 * j + 1).wait_recv()

        @pl.when(even & has_a)
        def _():
            send(C, 2 * j).start()
            send(C, 2 * j + 1).start()

        @pl.when(has_a)
        def _():
            whole(A, 2 * order(A, j, groups), 2, OWN, s_a, 1)

        @pl.when(odd & has_c)
        def _():
            send(C, 2 * j).wait_recv()
            send(C, 2 * j + 1).wait_recv()

        @pl.when(has_c)
        def _():
            whole(C, 2 * j, 2, OWN, s_c, 2)

        for now in range(groups):
            @pl.when(odd & has_a & has_c & (j == now))
            def _():
                some(C, 2 * now, 2, A, range(now + 1), s_c, 4)
                if now > 0:
                    some(A, 2 * order(A, now, groups), 2, C, range(now), s_a, 5)

        m = j - 1

        @pl.when(has_b & (j > 0))
        def _():
            send(B, 2 * m).wait_recv()
            send(B, 2 * m + 1).wait_recv()

            @pl.when(even)
            def _():
                whole(B, 2 * order(B, m, groups), 2, C, s_b, 4)

            for now in range(groups - 1):
                @pl.when(has_a & (m == now))
                def _():
                    some(B, 2 * order(B, now, groups), 2, A, range(min(now + 2, groups - now)), s_b, 3)

        return 0

    lax.fori_loop(0, groups, step, 0)

    def message(which, target):
        return pltpu.make_async_remote_copy(
            src_ref=msg.at[which], dst_ref=got.at[which], send_sem=msg_send.at[which],
            recv_sem=msg_recv.at[which], device_id=target, device_id_type=MESH)

    def masked(slot, tile, cluster, values):
        return jnp.where(row(slot, tile) == cluster, jnp.max(values, axis=0, keepdims=True), -1.0)

    def message_a(tile):
        msg[0, pl.ds(tile, 1), :] = jnp.maximum(
            jnp.maximum(masked(A, tile, s_a, pres[0, :, part(tile)]), masked(A, tile, s_b, qacc[3, :, part(tile)])),
            jnp.where(odd, masked(A, tile, s_c, qacc[4, :, part(tile)]), -1.0))

    def message_b(tile):
        msg[1, pl.ds(tile, 1), :] = masked(B, tile, s_b, pres[1, :, part(tile)])

    for tile in range(chunks):
        msg[2, tile:tile + 1, :] = jnp.maximum(
            masked(C, tile, s_c, pres[2, :, part(tile)]), jnp.where(odd, masked(C, tile, s_a, qacc[5, :, part(tile)]), -1.0))

    @pl.when(odd & has_c)
    def _():
        message(2, above).start()

    for tile in range(chunks):
        own = jnp.max(qacc[0, :, part(tile)], axis=0, keepdims=True)
        out_ref[tile:tile + 1, :] = jnp.maximum(
            jnp.maximum(own, -1.0),
            jnp.maximum(masked(OWN, tile, s_a, qacc[1, :, part(tile)]), masked(OWN, tile, s_c, qacc[2, :, part(tile)])))

    @pl.when(has_a & has_b)
    def _():
        some(B, 2 * order(B, 0, groups), 2, A, range(2, groups), s_b, 3)

    for t in range(2, chunks):
        message_a(order(A, t, chunks))
    for t in range(chunks - 2):
        message_b(order(B, t, chunks))

    def last_step(t, _):
        @pl.when(has_b)
        def _():
            send(B, t).wait_recv()

        @pl.when(has_a & has_b)
        def _():
            some(B, order(B, t, chunks), 1, A, range(1), s_b, 3)

        @pl.when(t == chunks - 1)
        def _():
            for i in range(2):
                message_a(order(A, i, chunks))

            @pl.when(has_a)
            def _():
                message(0, second).start()

        @pl.when(even & has_b)
        def _():
            whole(B, order(B, t, chunks), 1, C, s_b, 4)

        @pl.when(has_b)
        def _():
            message_b(order(B, t, chunks))

        return 0

    lax.fori_loop(chunks - 2, chunks, last_step, 0)

    @pl.when(has_b)
    def _():
        message(1, first).start()

    @pl.when(even)
    def _():
        for tile in range(chunks):
            msg[2, tile:tile + 1, :] = jnp.maximum(
                msg[2, tile:tile + 1, :], masked(C, tile, s_b, qacc[4, :, part(tile)]))
        message(2, above).start()

    messages = ((has_a, second, has_first), (has_b, first, has_second), (has_c, above, odd | has_down))
    @pl.when(has_first)
    def _():
        for t in range(LEAD, chunks):
            send(A, t).wait_send()

    @pl.when(has_second)
    def _():
        for t in range(chunks - OVER):
            send(B, t).wait_send()

    @pl.when(has_second & jnp.logical_not(over_r))
    def _():
        for t in range(chunks - OVER, chunks):
            send(B, t).wait_send()

    @pl.when(over_r)
    def _():
        for t in range(OVER):
            over(crossing, t, (OWN, relay), over_target).wait_send()

    @pl.when(over_next)
    def _():
        for t in range(OVER):
            over(0, t, (relay, relay), over_target).wait_send()

    @pl.when(over_y)
    def _():
        for i in range(crossings):
            for t in range(OVER):
                over(i, t, (relay, B), over_l_at(i)).wait_send()

    @pl.when(gives_c)
    def _():
        for t in range(chunks):
            send(C, t).wait_send()

    for which, (gives, target, gets) in enumerate(messages):
        @pl.when(gives)
        def _():
            message(which, target).wait_send()

        @pl.when(gets)
        def _():
            message(which, target).wait_recv()
            out_ref[...] = jnp.maximum(out_ref[...], got[which])


def shards(n_slab, n_member, embeddings, cluster_ids, keep_mask):
    rows, width = embeddings.shape
    chunks = rows // LANES
    crossings = n_slab * n_member // 2 // PLANE - 1
    highest = pl.pallas_call(
        functools.partial(kernel, n_slab, n_member),
        out_shape=jax.ShapeDtypeStruct((chunks, LANES), jnp.float32),
        in_specs=[pl.BlockSpec(memory_space=pltpu.HBM)] * 3,
        out_specs=pl.BlockSpec(memory_space=pltpu.VMEM),
        scratch_shapes=[
            pltpu.VMEM((rows, width), jnp.bfloat16),
            pltpu.VMEM((4, rows, width), jnp.bfloat16),
            pltpu.VMEM((4, 2 * chunks, LANES), jnp.int32),
            pltpu.VMEM((3, 8, rows), jnp.float32),
            pltpu.VMEM((6, 8, rows), jnp.float32),
            pltpu.VMEM((3, chunks, LANES), jnp.float32),
            pltpu.VMEM((3, chunks, LANES), jnp.float32),
            pltpu.VMEM((crossings, OVER, LANES, width), jnp.bfloat16),
            pltpu.SemaphoreType.DMA((chunks + 2,)),
            pltpu.SemaphoreType.DMA((4, chunks)),
            pltpu.SemaphoreType.DMA((4, chunks)),
            pltpu.SemaphoreType.DMA((4,)),
            pltpu.SemaphoreType.DMA((4,)),
            pltpu.SemaphoreType.DMA((3,)),
            pltpu.SemaphoreType.DMA((3,)),
            pltpu.SemaphoreType.DMA((crossings, OVER)),
            pltpu.SemaphoreType.DMA((crossings, OVER)),
            pltpu.SemaphoreType.REGULAR,
        ],
        compiler_params=pltpu.CompilerParams(
            collective_id=0, has_side_effects=True, vmem_limit_bytes=40 << 20),
    )(*(pltpu.with_memory_space_constraint(each, pltpu.HBM) for each in (
        embeddings, cluster_ids.reshape(chunks, LANES), keep_mask.reshape(chunks, LANES))))
    return highest.reshape(rows)


def solution(mesh):
    placed = (P(("slab", "member"), None), P(("slab", "member")), P(("slab", "member")))
    return jax.shard_map(
        functools.partial(shards, mesh.shape["slab"], mesh.shape["member"]),
        mesh=mesh, in_specs=placed, out_specs=P(("slab", "member")), check_vma=False,
    )
```

```python
import functools

import jax
import jax.numpy as jnp
from jax import lax
from jax.experimental import pallas as pl
from jax.experimental.pallas import tpu as pltpu
from jax.sharding import PartitionSpec as P

MESH = pl.DeviceIdType.MESH
OWN, A, B, C = 0, 1, 2, 3
LANES = 128
GROUP = 2 * LANES
LEAD = 5
MORE = 2
PLANE = 16
DOWN, UP = 3, 1
OUT = -4.0


def kernel(n_slab, n_member, x_ref, ids_ref, keep_ref, out_ref, raw, blk, tags, pres, qacc, msg, got,
           relay, load_sem, send_sem, recv_sem, tag_send, tag_recv, msg_send, msg_recv, over_send, over_recv, ready, early,
           edge_rows, edge_tags, edge_out, edge_got, edge_send, edge_recv):
    rows, width = raw.shape
    chunks, groups = rows // LANES, rows // GROUP
    count = n_slab * n_member
    slab, member = lax.axis_index("slab"), lax.axis_index("member")
    core = lax.rem(member, 2)
    place = slab * n_member + member
    chip = lax.div(place, 2)
    has_down, has_up = chip > 0, chip < count // 2 - 1
    even, odd = core == 0, core == 1

    def device(at):
        at = jnp.clip(at, 0, count - 1)
        return (lax.div(at, n_member), lax.rem(at, n_member))

    first, second = device(place - 2 + 4 * core), device(place + 2 - 4 * core)
    has_first = (even & has_down) | (odd & has_up)
    has_second = (even & has_up) | (odd & has_down)
    has_a, has_b, has_c = has_second, has_first, even | has_up
    gives_c = odd | has_up
    step_at = lax.rem(chip, PLANE)
    over_r, over_l = odd & (step_at == 0) & has_down, odd & (step_at == PLANE - 1) & has_up
    over_y = odd & (chip == count // 2 - 1)
    crossings = count // 2 // PLANE - 1
    crossing = lax.div(chip + 1, PLANE) - 1
    is_r, above_r = (step_at == 0) & has_down, (step_at == 1) & (chip > PLANE)
    over_first, over_next = over_r & (crossing == 0), over_r & (crossing == 1)
    over_to_y = over_r & jnp.logical_not(over_first)
    up_r, up_l = even & (step_at == 0) & has_down, even & (step_at == PLANE - 1) & has_up
    up_y = even & (chip == 0)
    up_mid, up_far = up_r & (crossing == 0), up_r & (crossing == 1)
    edge = even & (step_at == PLANE - 2) & (chip < count // 2 - PLANE)
    up_last, up_pass = up_l & (crossing == 2), up_l & (crossing == 1)
    c_source = jnp.where(even, A, OWN)
    sibling = (slab, member + 1 - 2 * core)
    above, below = device(place + 1), device(place - 1)

    barrier = pltpu.get_barrier_semaphore()
    partners = ((has_first, first), (has_second, second), (place < count - 1, above), (place > 0, below))
    told = partners + ((over_to_y | over_l, device(count - 1)), (over_next | up_far, device(place - 2 * PLANE)), (up_r & jnp.logical_not(up_far), device(0)))
    told = told + ((up_pass, device(place + 2 * PLANE)),)
    told = told + tuple((up_y, device(2 * (PLANE * (i + 1) - 1))) for i in range(crossings - 1))
    for there, other in told[:2]:
        @pl.when(there & jnp.logical_not(above_r & (odd if other is second else even)))
        def _():
            pl.semaphore_signal(barrier, inc=1, device_id=other, device_id_type=MESH)

    for there, other in told[2:]:
        @pl.when(there)
        def _():
            pl.semaphore_signal(barrier, inc=1, device_id=other, device_id_type=MESH)

    def part(t):
        return pl.ds(pl.multiple_of(t * LANES, LANES), LANES)

    def group_at(g):
        return pl.ds(pl.multiple_of(g * GROUP, GROUP), GROUP)

    def order(slot, t, count):
        if slot == C:
            return t
        flip = core if slot == A else 1 - core
        return t + flip * (count - 1 - 2 * t)

    def load(t):
        return pltpu.make_async_copy(x_ref.at[part(t)], raw.at[part(t)], load_sem.at[t])

    def send(slot, t):
        source, target = {A: (OWN, first), B: (OWN, second), C: (c_source, sibling)}[slot]
        rows_of = part(order(slot, t, chunks))
        return pltpu.make_async_remote_copy(
            src_ref=blk.at[source, rows_of], dst_ref=blk.at[slot, rows_of],
            send_sem=send_sem.at[slot, t], recv_sem=recv_sem.at[slot, t],
            device_id=target, device_id_type=MESH)

    def send_tags(src_slot, dst_slot, target):
        return pltpu.make_async_remote_copy(
            src_ref=tags.at[src_slot], dst_ref=tags.at[dst_slot], send_sem=tag_send.at[dst_slot],
            recv_sem=tag_recv.at[dst_slot], device_id=target, device_id_type=MESH)

    load_ids = pltpu.make_async_copy(ids_ref, tags.at[OWN, 0:chunks], load_sem.at[chunks])
    load_keep = pltpu.make_async_copy(keep_ref, tags.at[OWN, chunks:2 * chunks], load_sem.at[chunks + 1])
    load(order(A, 0, chunks)).start()
    load_ids.start()
    load_keep.start()
    for t in range(1, chunks):
        load(order(A, t, chunks)).start()
    for slot, there in ((A, has_a), (B, has_b), (C, has_c)):
        @pl.when(jnp.logical_not(there))
        def _():
            tags[slot] = jnp.full(tags.shape[1:], -2, jnp.int32)
    pres[...] = jnp.full(pres.shape, OUT, jnp.float32)
    qacc[...] = jnp.full(qacc.shape, OUT, jnp.float32)

    def normalise(t):
        load(t).wait()
        values = raw[part(t), :].astype(jnp.float32)
        scale = lax.rsqrt(jnp.sum(values * values, axis=1, keepdims=True) + 1e-06)
        blk[OWN, part(t), :] = (values * scale).astype(jnp.bfloat16)

    normalise(order(A, 0, chunks))
    load_ids.wait()
    load_keep.wait()
    tags[OWN, chunks:2 * chunks] = jnp.where(tags[OWN, chunks:2 * chunks] == 1, tags[OWN, 0:chunks], -1)
    heard = sum(there.astype(jnp.int32) for there, _ in partners)
    heard = heard + over_first.astype(jnp.int32) + over_y.astype(jnp.int32) * (2 * crossings - 1)
    heard = heard + (up_l | up_mid).astype(jnp.int32) + up_y.astype(jnp.int32) * (crossings - 1)
    heard = heard - is_r.astype(jnp.int32)

    @pl.when(jnp.logical_not(is_r))
    def _():
        pl.semaphore_wait(barrier, heard)

    @pl.when(above_r)
    def _():
        pl.semaphore_signal(early, inc=1, device_id=device(place - 2), device_id_type=MESH)

    @pl.when(is_r)
    def _():
        pl.semaphore_wait(early, 1)

    @pl.when(over_y)
    def _():
        for i in range(1, crossings):
            pl.semaphore_signal(ready, inc=1, device_id=device(2 * PLANE * (i + 1) + 1), device_id_type=MESH)

    first_now, second_now = has_first & jnp.logical_not(is_r & even), has_second & jnp.logical_not(is_r & odd)

    @pl.when(first_now)
    def _():
        send(A, 0).start()
        send_tags(OWN, A, first).start()

    @pl.when(second_now)
    def _():
        send_tags(OWN, B, second).start()

    def prepare(t, _):
        normalise(order(A, t, chunks))

        @pl.when(first_now)
        def _():
            send(A, t).start()

        return 0

    lax.fori_loop(1, chunks, prepare, 0)

    @pl.when(odd & jnp.logical_not(is_r))
    def _():
        for t in range(chunks):
            send(C, t).start()

    def row(slot, t):
        return tags[slot, pl.ds(t, 1), :]

    def columns(values):
        return jnp.broadcast_to(values, (LANES, LANES)).T

    def fold(values):
        return jnp.max(values.reshape(values.shape[0] // 8, 8, LANES), axis=0)

    def scores(p, q_slot, g):
        q = blk[q_slot, group_at(g), :]
        return lax.dot_general(p, q, (((1,), (1,)), ((), ())), preferred_element_type=jnp.float32)

    def own_step(t, _):
        p = blk[OWN, group_at(t), :]
        labels = jnp.concatenate(
            [columns(row(OWN, chunks + 2 * t + i).astype(jnp.float32)) for i in range(2)], axis=0)
        down = lax.broadcasted_iota(jnp.int32, (2 * LANES, LANES), 0) + t * 2 * LANES
        along = lax.broadcasted_iota(jnp.int32, (2 * LANES, LANES), 1)
        for n in range(chunks // 2):
            s = scores(p, OWN, n)
            for h in range(2):
                tile = 2 * n + h
                ids = row(OWN, tile).astype(jnp.float32)
                hits = (labels == ids) & (down != along + tile * LANES)
                top = fold(jnp.where(hits, s[:, h * LANES:(h + 1) * LANES], OUT))
                at = (0, slice(None), slice(tile * LANES, (tile + 1) * LANES))
                qacc[at] = jnp.maximum(qacc[at], top)
        return 0

    def shared(slot):
        low, high = tags[slot, 0:1, 0:1], tags[slot, chunks - 1:chunks, LANES - 1:LANES]
        if slot == C:
            return low
        return jnp.where(core == (0 if slot == A else 1), low, high)

    def biases(p_slot, t, size, cluster):
        each = [columns(jnp.where(row(p_slot, chunks + t + i) == cluster, 0.0, OUT)) for i in range(size)]
        return jnp.concatenate(each, axis=0) if size > 1 else each[0]

    def tile_pair(p, p_bias, best, q_slot, g, cluster, q_at):
        s = scores(p, q_slot, g)
        for h in range(2):
            one = s[:, h * LANES:(h + 1) * LANES]
            q_bias = jnp.where(row(q_slot, chunks + 2 * g + h) == cluster, 0.0, OUT)
            best = jnp.maximum(best, one + q_bias)
            at = (q_at, slice(None), part(2 * g + h))
            qacc[at] = jnp.maximum(qacc[at], fold(one + p_bias))
        return best

    def keep_rows(p_slot, t, size, best):
        for i in range(size):
            at = (p_slot - 1, slice(None), part(t + i))
            pres[at] = jnp.maximum(pres[at], fold(best[i * LANES:(i + 1) * LANES].T))

    def whole(p_slot, t, size, q_slot, cluster, q_at):
        p = blk[p_slot, pl.ds(pl.multiple_of(t * LANES, LANES), size * LANES), :]
        p_bias = biases(p_slot, t, size, cluster)
        best = jnp.full((size * LANES, LANES), OUT, jnp.float32)
        for g in range(groups):
            best = tile_pair(p, p_bias, best, q_slot, g, cluster, q_at)
        keep_rows(p_slot, t, size, best)

    def some(p_slot, t, size, q_slot, arrivals, cluster, q_at):
        p = blk[p_slot, pl.ds(pl.multiple_of(t * LANES, LANES), size * LANES), :]
        p_bias = biases(p_slot, t, size, cluster)
        best = jnp.full((size * LANES, LANES), OUT, jnp.float32)
        for i in arrivals:
            best = tile_pair(p, p_bias, best, q_slot, order(q_slot, i, groups), cluster, q_at)
        keep_rows(p_slot, t, size, best)

    over_target = device(jnp.where(even, jnp.where(up_last, place - 2 * PLANE, 0), jnp.where(crossing == 0, place + 2 * PLANE, count - 1)))

    def l_at(i):
        return device(2 * (PLANE * (i + 1) - 1) + core)

    def r_at(i):
        return device(2 * PLANE * (i + 1) + core)

    def over(total, i, t, way, target):
        source, there = way
        rows_of = part(order(B, chunks - total + t, chunks))
        return pltpu.make_async_remote_copy(
            src_ref=relay.at[i, t] if source is relay else blk.at[OWN, rows_of],
            dst_ref=relay.at[i, t] if there is relay else blk.at[B, rows_of],
            send_sem=over_send.at[i, t],
            recv_sem=over_recv.at[i, t] if there is relay else recv_sem.at[B, chunks - total + t],
            device_id=target, device_id_type=MESH)

    @pl.when(up_l)
    def _():
        for t in range(UP):
            over(UP, crossing, t, (OWN, relay), over_target).start()

    lax.fori_loop(0, groups, own_step, 0)

    @pl.when(is_r)
    def _():
        pl.semaphore_wait(barrier, heard)

    @pl.when(is_r & even)
    def _():
        send_tags(OWN, A, first).start()
        for t in range(chunks):
            send(A, t).start()

    @pl.when(is_r & odd)
    def _():
        send_tags(OWN, B, second).start()
        for t in range(chunks):
            send(C, t).start()

    @pl.when(over_first)
    def _():
        for t in range(DOWN):
            over(DOWN, crossing, t, (OWN, relay), over_target).start()


    @pl.when(over_to_y)
    def _():
        pl.semaphore_wait(ready, 1)
        for t in range(DOWN):
            over(DOWN, crossing, t, (OWN, relay), over_target).start()

    @pl.when(up_pass)
    def _():
        for t in range(UP):
            over(UP, 2, t, (OWN, relay), first).wait_recv()
            over(UP, 2, t, (relay, relay), over_target).start()

    @pl.when(over_next)
    def _():
        for t in range(DOWN):
            over(DOWN, 0, t, (OWN, relay), first).wait_recv()
            over(DOWN, 0, t, (relay, relay), over_target).start()

    @pl.when(has_first)
    def _():
        for t in range(LEAD):
            send(A, t).wait_send()

    @pl.when(is_r & odd)
    def _():
        for t in range(LEAD, LEAD + MORE):
            send(A, t).wait_send()

    @pl.when(has_second)
    def _():
        for t in range(chunks - DOWN):
            send(B, t).start()

    @pl.when(has_second & jnp.logical_not(over_r))
    def _():
        for t in range(chunks - DOWN, chunks - UP):
            send(B, t).start()

    @pl.when(has_second & jnp.logical_not(over_r | up_l))
    def _():
        for t in range(chunks - UP, chunks):
            send(B, t).start()

    @pl.when(has_first)
    def _():
        send_tags(OWN, A, first).wait_send()

    @pl.when(has_second)
    def _():
        send_tags(OWN, B, second).wait_send()

    @pl.when(has_a)
    def _():
        send_tags(OWN, A, first).wait_recv()

    @pl.when(has_b)
    def _():
        send_tags(OWN, B, second).wait_recv()

    @pl.when(gives_c)
    def _():
        send_tags(c_source, C, sibling).start()
        send_tags(c_source, C, sibling).wait_send()

    @pl.when(has_c)
    def _():
        send_tags(c_source, C, sibling).wait_recv()

    s_a, s_b, s_c = shared(A), shared(B), shared(C)

    @pl.when(even)
    def _():
        for t in range(chunks):
            send(C, t).wait_recv()

    def edge_copies():
        return (
            pltpu.make_async_remote_copy(
                src_ref=blk.at[A, part(0)], dst_ref=edge_rows, send_sem=edge_send.at[0], recv_sem=edge_recv.at[0],
                device_id=first, device_id_type=MESH),
            pltpu.make_async_remote_copy(
                src_ref=tags.at[A], dst_ref=edge_tags, send_sem=edge_send.at[1], recv_sem=edge_recv.at[1],
                device_id=first, device_id_type=MESH))

    def edge_message():
        return pltpu.make_async_remote_copy(
            src_ref=edge_out, dst_ref=edge_got, send_sem=edge_send.at[2], recv_sem=edge_recv.at[2],
            device_id=second, device_id_type=MESH)

    def step(j, _):
        @pl.when(up_mid & (j == groups - 1))
        def _():
            for t in range(UP):
                over(UP, 1, t, (OWN, relay), first).wait_recv()
                over(UP, 1, t, (relay, B), r_at(1)).start()

        @pl.when(over_y & (j == groups - 3))
        def _():
            for i in range(crossings):
                for t in range(DOWN):
                    over(DOWN, i, t, (OWN, relay), first).wait_recv()
                    over(DOWN, i, t, (relay, B), l_at(i)).start()

        @pl.when(up_y & (j == groups - 2))
        def _():
            for i in (1, 0, 2):
                for t in range(UP):
                    over(UP, i, t, (OWN, relay), first).wait_recv()
                    over(UP, i, t, (relay, relay if i == 1 else B), r_at(0 if i == 1 else i)).start()

        @pl.when(has_a)
        def _():
            send(A, 2 * j).wait_recv()
            send(A, 2 * j + 1).wait_recv()

        @pl.when(even & has_a)
        def _():
            send(C, 2 * j).start()
            send(C, 2 * j + 1).start()

        @pl.when(up_l & (j == 0))
        def _():
            for each in edge_copies():
                each.start()

        @pl.when(has_a)
        def _():
            whole(A, 2 * order(A, j, groups), 2, OWN, s_a, 1)

        @pl.when(odd & has_c)
        def _():
            send(C, 2 * j).wait_recv()
            send(C, 2 * j + 1).wait_recv()

        @pl.when(has_c)
        def _():
            whole(C, 2 * j, 2, OWN, s_c, 2)

        for now in range(groups):
            @pl.when(odd & has_a & has_c & (j == now))
            def _():
                some(C, 2 * now, 2, A, range(now + 1), s_c, 4)
                if now > 0:
                    some(A, 2 * order(A, now, groups), 2, C, range(now), s_a, 5)

        m = j - 1

        @pl.when(has_b & (j > 0) & (j < groups - 1))
        def _():
            send(B, 2 * m).wait_recv()
            send(B, 2 * m + 1).wait_recv()

            @pl.when(even)
            def _():
                whole(B, 2 * order(B, m, groups), 2, C, s_b, 4)

            for now in range(groups - 2):
                @pl.when(has_a & (m == now))
                def _():
                    some(B, 2 * order(B, now, groups), 2, A, range(min(now + 2, groups - now)), s_b, 3)

        return 0

    lax.fori_loop(0, groups, step, 0)

    def message(which, target):
        return pltpu.make_async_remote_copy(
            src_ref=msg.at[which], dst_ref=got.at[which], send_sem=msg_send.at[which],
            recv_sem=msg_recv.at[which], device_id=target, device_id_type=MESH)

    def masked(slot, tile, cluster, values):
        return jnp.where(row(slot, tile) == cluster, jnp.max(values, axis=0, keepdims=True), -1.0)

    def message_a(tile):
        msg[0, pl.ds(tile, 1), :] = jnp.maximum(
            jnp.maximum(masked(A, tile, s_a, pres[0, :, part(tile)]), masked(A, tile, s_b, qacc[3, :, part(tile)])),
            jnp.where(odd, masked(A, tile, s_c, qacc[4, :, part(tile)]), -1.0))

    def message_b(tile):
        msg[1, pl.ds(tile, 1), :] = masked(B, tile, s_b, pres[1, :, part(tile)])

    for tile in range(chunks):
        msg[2, tile:tile + 1, :] = jnp.maximum(
            masked(C, tile, s_c, pres[2, :, part(tile)]), jnp.where(odd, masked(C, tile, s_a, qacc[5, :, part(tile)]), -1.0))

    @pl.when(odd & has_c)
    def _():
        message(2, above).start()

    for tile in range(chunks):
        own = jnp.max(qacc[0, :, part(tile)], axis=0, keepdims=True)
        out_ref[tile:tile + 1, :] = jnp.maximum(
            jnp.maximum(own, -1.0),
            jnp.maximum(masked(OWN, tile, s_a, qacc[1, :, part(tile)]), masked(OWN, tile, s_c, qacc[2, :, part(tile)])))

    @pl.when(edge)
    def _():
        for each in edge_copies():
            each.wait_recv()
        cluster = edge_tags[0:1, 0:1]
        s = lax.dot_general(
            edge_rows[...], blk[OWN, part(0), :], (((1,), (1,)), ((), ())), preferred_element_type=jnp.float32)
        p_bias = columns(jnp.where(edge_tags[chunks:chunks + 1, :] == cluster, 0.0, OUT))
        q_bias = jnp.where(row(OWN, chunks) == cluster, 0.0, OUT)
        rows_best = jnp.max((s + q_bias).T, axis=0, keepdims=True)
        edge_out[...] = jnp.broadcast_to(jnp.where(edge_tags[0:1, :] == cluster, rows_best, -1.0), edge_out.shape)
        edge_message().start()
        own_best = jnp.max(s + p_bias, axis=0, keepdims=True)
        out_ref[0:1, :] = jnp.maximum(out_ref[0:1, :], jnp.where(row(OWN, 0) == cluster, own_best, -1.0))

    @pl.when(has_a & has_b)
    def _():
        some(B, 2 * order(B, 0, groups), 2, A, range(2, groups), s_b, 3)

    for t in range(4, chunks):
        message_a(order(A, t, chunks))
    for t in range(chunks - 4):
        message_b(order(B, t, chunks))

    @pl.when(over_l)
    def _():
        for t in range(chunks - 2, chunks):
            send(B, t).wait_recv()
        some(B, 2 * order(B, groups - 1, groups), 2, A, range(1), s_b, 3)
        for t in range(chunks - 2, chunks):
            message_b(order(B, t, chunks))

    @pl.when(has_b)
    def _():
        m = groups - 2
        send(B, 2 * m).wait_recv()
        send(B, 2 * m + 1).wait_recv()

        @pl.when(has_a)
        def _():
            some(B, 2 * order(B, m, groups), 2, A, range(groups - m), s_b, 3)

        @pl.when(even)
        def _():
            whole(B, 2 * order(B, m, groups), 2, C, s_b, 4)

    for t in range(chunks - 4, chunks - 2):
        message_b(order(B, t, chunks))

    @pl.when(over_l)
    def _():
        message(1, first).start()

    for t in range(2, 4):
        message_a(order(A, t, chunks))

    def last_step(i, _):
        t = i + up_r.astype(jnp.int32) * (2 * chunks - 3 - 2 * i)

        comes = has_b & jnp.logical_not(over_l)

        @pl.when(comes)
        def _():
            send(B, t).wait_recv()

        @pl.when(has_a & comes)
        def _():
            some(B, order(B, t, chunks), 1, A, range(1), s_b, 3)

        @pl.when(odd & comes)
        def _():
            message_b(order(B, t, chunks))

        @pl.when(odd & comes & (i == chunks - 1))
        def _():
            message(1, first).start()

        @pl.when(i == jnp.where(up_l, chunks - 2, chunks - 1))
        def _():
            for each in range(2):
                message_a(order(A, each, chunks))

            @pl.when(up_l)
            def _():
                edge_message().wait_recv()
                msg[0, 0:1, :] = jnp.maximum(msg[0, 0:1, :], edge_got[0:1, :])

            @pl.when(has_a)
            def _():
                message(0, second).start()

        @pl.when(even & has_b)
        def _():
            whole(B, order(B, t, chunks), 1, C, s_b, 4)

        @pl.when(even & has_b)
        def _():
            message_b(order(B, t, chunks))

        return 0

    lax.fori_loop(chunks - 2, chunks, last_step, 0)

    @pl.when(even & has_b)
    def _():
        message(1, first).start()

    @pl.when(even)
    def _():
        for tile in range(chunks):
            msg[2, tile:tile + 1, :] = jnp.maximum(
                msg[2, tile:tile + 1, :], masked(C, tile, s_b, qacc[4, :, part(tile)]))
        message(2, above).start()

    messages = ((has_a, second, has_first), (has_b, first, has_second), (has_c, above, odd | has_down))
    @pl.when(has_first)
    def _():
        for t in range(LEAD + MORE, chunks):
            send(A, t).wait_send()

    @pl.when(has_first & jnp.logical_not(is_r & odd))
    def _():
        for t in range(LEAD, LEAD + MORE):
            send(A, t).wait_send()

    @pl.when(has_second)
    def _():
        for t in range(chunks - DOWN):
            send(B, t).wait_send()

    @pl.when(has_second & jnp.logical_not(over_r))
    def _():
        for t in range(chunks - DOWN, chunks - UP):
            send(B, t).wait_send()

    @pl.when(has_second & jnp.logical_not(over_r | up_l))
    def _():
        for t in range(chunks - UP, chunks):
            send(B, t).wait_send()

    @pl.when(over_r)
    def _():
        for t in range(DOWN):
            over(DOWN, crossing, t, (OWN, relay), over_target).wait_send()

    @pl.when(over_next)
    def _():
        for t in range(DOWN):
            over(DOWN, 0, t, (relay, relay), over_target).wait_send()

    @pl.when(over_y)
    def _():
        for i in range(crossings):
            for t in range(DOWN):
                over(DOWN, i, t, (relay, B), l_at(i)).wait_send()

    @pl.when(up_l)
    def _():
        for t in range(UP):
            over(UP, crossing, t, (OWN, relay), over_target).wait_send()

    @pl.when(up_pass)
    def _():
        for t in range(UP):
            over(UP, 2, t, (relay, relay), over_target).wait_send()

    @pl.when(up_mid)
    def _():
        for t in range(UP):
            over(UP, 1, t, (relay, B), r_at(1)).wait_send()

    @pl.when(up_y)
    def _():
        for i in range(crossings):
            for t in range(UP):
                over(UP, i, t, (relay, relay if i == 1 else B), r_at(0 if i == 1 else i)).wait_send()

    @pl.when(gives_c)
    def _():
        for t in range(chunks):
            send(C, t).wait_send()

    @pl.when(up_l)
    def _():
        for each in edge_copies():
            each.wait_send()

    @pl.when(edge)
    def _():
        edge_message().wait_send()

    for which, (gives, target, gets) in enumerate(messages):
        @pl.when(gives)
        def _():
            message(which, target).wait_send()

        @pl.when(gets)
        def _():
            message(which, target).wait_recv()
            out_ref[...] = jnp.maximum(out_ref[...], got[which])


def shards(n_slab, n_member, embeddings, cluster_ids, keep_mask):
    rows, width = embeddings.shape
    chunks = rows // LANES
    crossings = n_slab * n_member // 2 // PLANE - 1
    highest = pl.pallas_call(
        functools.partial(kernel, n_slab, n_member),
        out_shape=jax.ShapeDtypeStruct((chunks, LANES), jnp.float32),
        in_specs=[pl.BlockSpec(memory_space=pltpu.HBM)] * 3,
        out_specs=pl.BlockSpec(memory_space=pltpu.VMEM),
        scratch_shapes=[
            pltpu.VMEM((rows, width), jnp.bfloat16),
            pltpu.VMEM((4, rows, width), jnp.bfloat16),
            pltpu.VMEM((4, 2 * chunks, LANES), jnp.int32),
            pltpu.VMEM((3, 8, rows), jnp.float32),
            pltpu.VMEM((6, 8, rows), jnp.float32),
            pltpu.VMEM((3, chunks, LANES), jnp.float32),
            pltpu.VMEM((3, chunks, LANES), jnp.float32),
            pltpu.VMEM((crossings, DOWN, LANES, width), jnp.bfloat16),
            pltpu.SemaphoreType.DMA((chunks + 2,)),
            pltpu.SemaphoreType.DMA((4, chunks)),
            pltpu.SemaphoreType.DMA((4, chunks)),
            pltpu.SemaphoreType.DMA((4,)),
            pltpu.SemaphoreType.DMA((4,)),
            pltpu.SemaphoreType.DMA((3,)),
            pltpu.SemaphoreType.DMA((3,)),
            pltpu.SemaphoreType.DMA((crossings, DOWN)),
            pltpu.SemaphoreType.DMA((crossings, DOWN)),
            pltpu.SemaphoreType.REGULAR,
            pltpu.SemaphoreType.REGULAR,
            pltpu.VMEM((LANES, width), jnp.bfloat16),
            pltpu.VMEM((2 * chunks, LANES), jnp.int32),
            pltpu.VMEM((8, LANES), jnp.float32),
            pltpu.VMEM((8, LANES), jnp.float32),
            pltpu.SemaphoreType.DMA((3,)),
            pltpu.SemaphoreType.DMA((3,)),
        ],
        compiler_params=pltpu.CompilerParams(
            collective_id=0, has_side_effects=True, vmem_limit_bytes=40 << 20),
    )(*(pltpu.with_memory_space_constraint(each, pltpu.HBM) for each in (
        embeddings, cluster_ids.reshape(chunks, LANES), keep_mask.reshape(chunks, LANES))))
    return highest.reshape(rows)


def solution(mesh):
    placed = (P(("slab", "member"), None), P(("slab", "member")), P(("slab", "member")))
    return jax.shard_map(
        functools.partial(shards, mesh.shape["slab"], mesh.shape["member"]),
        mesh=mesh, in_specs=placed, out_specs=P(("slab", "member")), check_vma=False,
    )
```

```python
import functools

import jax
import jax.numpy as jnp
from jax import lax
from jax.experimental import pallas as pl
from jax.experimental.pallas import tpu as pltpu
from jax.sharding import PartitionSpec as P

MESH = pl.DeviceIdType.MESH
OWN, A, B, C = 0, 1, 2, 3
LANES = 128
GROUP = 2 * LANES
LEAD = 5
MORE = 2
PLANE = 16
DOWN, UP = 3, 1
OUT = -4.0


def kernel(n_slab, n_member, x_ref, ids_ref, keep_ref, out_ref, raw, blk, tags, pres, qacc, msg, got,
           relay, load_sem, send_sem, recv_sem, tag_send, tag_recv, msg_send, msg_recv, over_send, over_recv, ready, early,
           edge_rows, edge_tags, edge_out, edge_got, edge_send, edge_recv):
    rows, width = raw.shape
    chunks, groups = rows // LANES, rows // GROUP
    count = n_slab * n_member
    slab, member = lax.axis_index("slab"), lax.axis_index("member")
    core = lax.rem(member, 2)
    place = slab * n_member + member
    chip = lax.div(place, 2)
    has_down, has_up = chip > 0, chip < count // 2 - 1
    even, odd = core == 0, core == 1

    def device(at):
        at = jnp.clip(at, 0, count - 1)
        return (lax.div(at, n_member), lax.rem(at, n_member))

    first, second = device(place - 2 + 4 * core), device(place + 2 - 4 * core)
    has_first = (even & has_down) | (odd & has_up)
    has_second = (even & has_up) | (odd & has_down)
    has_a, has_b, has_c = has_second, has_first, even | has_up
    gives_c = odd | has_up
    step_at = lax.rem(chip, PLANE)
    over_r, over_l = odd & (step_at == 0) & has_down, odd & (step_at == PLANE - 1) & has_up
    over_y = odd & (chip == count // 2 - 1)
    crossings = count // 2 // PLANE - 1
    crossing = lax.div(chip + 1, PLANE) - 1
    is_r, above_r = (step_at == 0) & has_down, (step_at == 1) & (chip > PLANE)
    over_first, over_next = over_r & (crossing == 0), over_r & (crossing == 1)
    over_to_y = over_r & jnp.logical_not(over_first)
    up_r, up_l = even & (step_at == 0) & has_down, even & (step_at == PLANE - 1) & has_up
    up_y = even & (chip == 0)
    up_mid, up_far = up_r & (crossing == 0), up_r & (crossing == 1)
    edge = even & (step_at == PLANE - 2) & (chip < count // 2 - PLANE)
    up_last, up_pass = up_l & (crossing == 2), up_l & (crossing == 1)
    c_source = jnp.where(even, A, OWN)
    sibling = (slab, member + 1 - 2 * core)
    above, below = device(place + 1), device(place - 1)

    barrier = pltpu.get_barrier_semaphore()
    partners = ((has_first, first), (has_second, second), (place < count - 1, above), (place > 0, below))
    told = partners + ((over_to_y | over_l, device(count - 1)), (over_next | up_far, device(place - 2 * PLANE)), (up_r & jnp.logical_not(up_far), device(0)))
    told = told + ((up_pass, device(place + 2 * PLANE)),)
    told = told + tuple((up_y, device(2 * (PLANE * (i + 1) - 1))) for i in range(crossings - 1))
    for there, other in told[:2]:
        @pl.when(there & jnp.logical_not(above_r & (odd if other is second else even)))
        def _():
            pl.semaphore_signal(barrier, inc=1, device_id=other, device_id_type=MESH)

    for there, other in told[2:]:
        @pl.when(there)
        def _():
            pl.semaphore_signal(barrier, inc=1, device_id=other, device_id_type=MESH)

    def part(t):
        return pl.ds(pl.multiple_of(t * LANES, LANES), LANES)

    def group_at(g):
        return pl.ds(pl.multiple_of(g * GROUP, GROUP), GROUP)

    def order(slot, t, count):
        if slot == C:
            return t
        flip = core if slot == A else 1 - core
        return t + flip * (count - 1 - 2 * t)

    def load(t):
        return pltpu.make_async_copy(x_ref.at[part(t)], raw.at[part(t)], load_sem.at[t])

    def send(slot, t):
        source, target = {A: (OWN, first), B: (OWN, second), C: (c_source, sibling)}[slot]
        rows_of = part(order(slot, t, chunks))
        return pltpu.make_async_remote_copy(
            src_ref=blk.at[source, rows_of], dst_ref=blk.at[slot, rows_of],
            send_sem=send_sem.at[slot, t], recv_sem=recv_sem.at[slot, t],
            device_id=target, device_id_type=MESH)

    def send_tags(src_slot, dst_slot, target):
        return pltpu.make_async_remote_copy(
            src_ref=tags.at[src_slot], dst_ref=tags.at[dst_slot], send_sem=tag_send.at[dst_slot],
            recv_sem=tag_recv.at[dst_slot], device_id=target, device_id_type=MESH)

    load_ids = pltpu.make_async_copy(ids_ref, tags.at[OWN, 0:chunks], load_sem.at[chunks])
    load_keep = pltpu.make_async_copy(keep_ref, tags.at[OWN, chunks:2 * chunks], load_sem.at[chunks + 1])
    load(order(A, 0, chunks)).start()
    load_ids.start()
    load_keep.start()
    for t in range(1, chunks):
        load(order(A, t, chunks)).start()
    for slot, there in ((A, has_a), (B, has_b), (C, has_c)):
        @pl.when(jnp.logical_not(there))
        def _():
            tags[slot] = jnp.full(tags.shape[1:], -2, jnp.int32)
    pres[...] = jnp.full(pres.shape, OUT, jnp.float32)
    qacc[...] = jnp.full(qacc.shape, OUT, jnp.float32)

    def normalise(t):
        load(t).wait()
        values = raw[part(t), :].astype(jnp.float32)
        scale = lax.rsqrt(jnp.sum(values * values, axis=1, keepdims=True) + 1e-06)
        blk[OWN, part(t), :] = (values * scale).astype(jnp.bfloat16)

    normalise(order(A, 0, chunks))
    load_ids.wait()
    load_keep.wait()
    tags[OWN, chunks:2 * chunks] = jnp.where(tags[OWN, chunks:2 * chunks] == 1, tags[OWN, 0:chunks], -1)
    heard = sum(there.astype(jnp.int32) for there, _ in partners)
    heard = heard + over_first.astype(jnp.int32) + over_y.astype(jnp.int32) * (2 * crossings - 1)
    heard = heard + (up_l | up_mid).astype(jnp.int32) + up_y.astype(jnp.int32) * (crossings - 1)
    heard = heard - is_r.astype(jnp.int32)

    @pl.when(jnp.logical_not(is_r))
    def _():
        pl.semaphore_wait(barrier, heard)

    @pl.when(above_r)
    def _():
        pl.semaphore_signal(early, inc=1, device_id=device(place - 2), device_id_type=MESH)

    @pl.when(is_r)
    def _():
        pl.semaphore_wait(early, 1)

    @pl.when(over_y)
    def _():
        for i in range(1, crossings):
            pl.semaphore_signal(ready, inc=1, device_id=device(2 * PLANE * (i + 1) + 1), device_id_type=MESH)

    first_now, second_now = has_first & jnp.logical_not(is_r & even), has_second & jnp.logical_not(is_r & odd)

    @pl.when(first_now)
    def _():
        send(A, 0).start()
        send_tags(OWN, A, first).start()

    @pl.when(second_now)
    def _():
        send_tags(OWN, B, second).start()

    def prepare(t, _):
        normalise(order(A, t, chunks))

        @pl.when(first_now)
        def _():
            send(A, t).start()

        return 0

    lax.fori_loop(1, chunks, prepare, 0)

    @pl.when(odd & jnp.logical_not(is_r))
    def _():
        for t in range(chunks):
            send(C, t).start()

    def row(slot, t):
        return tags[slot, pl.ds(t, 1), :]

    def columns(values):
        return jnp.broadcast_to(values, (LANES, LANES)).T

    def fold(values):
        return jnp.max(values.reshape(values.shape[0] // 8, 8, LANES), axis=0)

    def scores(p, q_slot, g):
        q = blk[q_slot, group_at(g), :]
        return lax.dot_general(p, q, (((1,), (1,)), ((), ())), preferred_element_type=jnp.float32)

    def own_step(t, _):
        p = blk[OWN, group_at(t), :]
        labels = jnp.concatenate(
            [columns(row(OWN, chunks + 2 * t + i).astype(jnp.float32)) for i in range(2)], axis=0)
        down = lax.broadcasted_iota(jnp.int32, (2 * LANES, LANES), 0) + t * 2 * LANES
        along = lax.broadcasted_iota(jnp.int32, (2 * LANES, LANES), 1)
        for n in range(chunks // 2):
            s = scores(p, OWN, n)
            for h in range(2):
                tile = 2 * n + h
                ids = row(OWN, tile).astype(jnp.float32)
                hits = (labels == ids) & (down != along + tile * LANES)
                top = fold(jnp.where(hits, s[:, h * LANES:(h + 1) * LANES], OUT))
                at = (0, slice(None), slice(tile * LANES, (tile + 1) * LANES))
                qacc[at] = jnp.maximum(qacc[at], top)
        return 0

    def shared(slot):
        low, high = tags[slot, 0:1, 0:1], tags[slot, chunks - 1:chunks, LANES - 1:LANES]
        if slot == C:
            return low
        return jnp.where(core == (0 if slot == A else 1), low, high)

    def biases(p_slot, t, size, cluster):
        each = [columns(jnp.where(row(p_slot, chunks + t + i) == cluster, 0.0, OUT)) for i in range(size)]
        return jnp.concatenate(each, axis=0) if size > 1 else each[0]

    def tile_pair(p, p_bias, best, q_slot, g, cluster, q_at):
        s = scores(p, q_slot, g)
        for h in range(2):
            one = s[:, h * LANES:(h + 1) * LANES]
            q_bias = jnp.where(row(q_slot, chunks + 2 * g + h) == cluster, 0.0, OUT)
            best = jnp.maximum(best, one + q_bias)
            at = (q_at, slice(None), part(2 * g + h))
            qacc[at] = jnp.maximum(qacc[at], fold(one + p_bias))
        return best

    def keep_rows(p_slot, t, size, best):
        for i in range(size):
            at = (p_slot - 1, slice(None), part(t + i))
            pres[at] = jnp.maximum(pres[at], fold(best[i * LANES:(i + 1) * LANES].T))

    def whole(p_slot, t, size, q_slot, cluster, q_at):
        p = blk[p_slot, pl.ds(pl.multiple_of(t * LANES, LANES), size * LANES), :]
        p_bias = biases(p_slot, t, size, cluster)
        best = jnp.full((size * LANES, LANES), OUT, jnp.float32)
        for g in range(groups):
            best = tile_pair(p, p_bias, best, q_slot, g, cluster, q_at)
        keep_rows(p_slot, t, size, best)

    def some(p_slot, t, size, q_slot, arrivals, cluster, q_at):
        p = blk[p_slot, pl.ds(pl.multiple_of(t * LANES, LANES), size * LANES), :]
        p_bias = biases(p_slot, t, size, cluster)
        best = jnp.full((size * LANES, LANES), OUT, jnp.float32)
        for i in arrivals:
            best = tile_pair(p, p_bias, best, q_slot, order(q_slot, i, groups), cluster, q_at)
        keep_rows(p_slot, t, size, best)

    over_target = device(jnp.where(even, jnp.where(up_last, place - 2 * PLANE, 0), jnp.where(crossing == 0, place + 2 * PLANE, count - 1)))

    def l_at(i):
        return device(2 * (PLANE * (i + 1) - 1) + core)

    def r_at(i):
        return device(2 * PLANE * (i + 1) + core)

    def over(total, i, t, way, target):
        source, there = way
        rows_of = part(order(B, chunks - total + t, chunks))
        return pltpu.make_async_remote_copy(
            src_ref=relay.at[i, t] if source is relay else blk.at[OWN, rows_of],
            dst_ref=relay.at[i, t] if there is relay else blk.at[B, rows_of],
            send_sem=over_send.at[i, t],
            recv_sem=over_recv.at[i, t] if there is relay else recv_sem.at[B, chunks - total + t],
            device_id=target, device_id_type=MESH)

    @pl.when(up_l)
    def _():
        for t in range(UP):
            over(UP, crossing, t, (OWN, relay), over_target).start()

    @pl.when(is_r)
    def _():
        pl.semaphore_wait(barrier, heard)

    @pl.when(is_r & even)
    def _():
        send_tags(OWN, A, first).start()
        for t in range(chunks):
            send(A, t).start()

    @pl.when(is_r & odd)
    def _():
        send_tags(OWN, B, second).start()
        for t in range(chunks):
            send(C, t).start()

    @pl.when(over_first)
    def _():
        for t in range(DOWN):
            over(DOWN, crossing, t, (OWN, relay), over_target).start()


    lax.fori_loop(0, groups, own_step, 0)

    @pl.when(over_to_y)
    def _():
        pl.semaphore_wait(ready, 1)
        for t in range(DOWN):
            over(DOWN, crossing, t, (OWN, relay), over_target).start()

    @pl.when(up_pass)
    def _():
        for t in range(UP):
            over(UP, 2, t, (OWN, relay), first).wait_recv()
            over(UP, 2, t, (relay, relay), over_target).start()

    @pl.when(over_next)
    def _():
        for t in range(DOWN):
            over(DOWN, 0, t, (OWN, relay), first).wait_recv()
            over(DOWN, 0, t, (relay, relay), over_target).start()

    @pl.when(has_first)
    def _():
        for t in range(LEAD):
            send(A, t).wait_send()

    @pl.when(is_r & odd)
    def _():
        for t in range(LEAD, LEAD + MORE):
            send(A, t).wait_send()

    @pl.when(has_second)
    def _():
        for t in range(chunks - DOWN):
            send(B, t).start()

    @pl.when(has_second & jnp.logical_not(over_r))
    def _():
        for t in range(chunks - DOWN, chunks - UP):
            send(B, t).start()

    @pl.when(has_second & jnp.logical_not(over_r | up_l))
    def _():
        for t in range(chunks - UP, chunks):
            send(B, t).start()

    @pl.when(has_first)
    def _():
        send_tags(OWN, A, first).wait_send()

    @pl.when(has_second)
    def _():
        send_tags(OWN, B, second).wait_send()

    @pl.when(has_a)
    def _():
        send_tags(OWN, A, first).wait_recv()

    @pl.when(has_b)
    def _():
        send_tags(OWN, B, second).wait_recv()

    @pl.when(gives_c)
    def _():
        send_tags(c_source, C, sibling).start()
        send_tags(c_source, C, sibling).wait_send()

    @pl.when(has_c)
    def _():
        send_tags(c_source, C, sibling).wait_recv()

    s_a, s_b, s_c = shared(A), shared(B), shared(C)

    @pl.when(even)
    def _():
        for t in range(chunks):
            send(C, t).wait_recv()

    def edge_copies():
        return (
            pltpu.make_async_remote_copy(
                src_ref=blk.at[A, part(0)], dst_ref=edge_rows, send_sem=edge_send.at[0], recv_sem=edge_recv.at[0],
                device_id=first, device_id_type=MESH),
            pltpu.make_async_remote_copy(
                src_ref=tags.at[A], dst_ref=edge_tags, send_sem=edge_send.at[1], recv_sem=edge_recv.at[1],
                device_id=first, device_id_type=MESH))

    def edge_message():
        return pltpu.make_async_remote_copy(
            src_ref=edge_out, dst_ref=edge_got, send_sem=edge_send.at[2], recv_sem=edge_recv.at[2],
            device_id=second, device_id_type=MESH)

    def step(j, _):
        @pl.when(up_mid & (j == groups - 1))
        def _():
            for t in range(UP):
                over(UP, 1, t, (OWN, relay), first).wait_recv()
                over(UP, 1, t, (relay, B), r_at(1)).start()

        @pl.when(over_y & (j == groups - 3))
        def _():
            for i in range(crossings):
                for t in range(DOWN):
                    over(DOWN, i, t, (OWN, relay), first).wait_recv()
                    over(DOWN, i, t, (relay, B), l_at(i)).start()

        @pl.when(up_y & (j == groups - 2))
        def _():
            for i in (1, 0, 2):
                for t in range(UP):
                    over(UP, i, t, (OWN, relay), first).wait_recv()
                    over(UP, i, t, (relay, relay if i == 1 else B), r_at(0 if i == 1 else i)).start()

        @pl.when(has_a)
        def _():
            send(A, 2 * j).wait_recv()
            send(A, 2 * j + 1).wait_recv()

        @pl.when(even & has_a)
        def _():
            send(C, 2 * j).start()
            send(C, 2 * j + 1).start()

        @pl.when(up_l & (j == 0))
        def _():
            for each in edge_copies():
                each.start()

        @pl.when(has_a)
        def _():
            whole(A, 2 * order(A, j, groups), 2, OWN, s_a, 1)

        @pl.when(odd & has_c)
        def _():
            send(C, 2 * j).wait_recv()
            send(C, 2 * j + 1).wait_recv()

        @pl.when(has_c)
        def _():
            whole(C, 2 * j, 2, OWN, s_c, 2)

        for now in range(groups):
            @pl.when(odd & has_a & has_c & (j == now))
            def _():
                some(C, 2 * now, 2, A, range(now + 1), s_c, 4)
                if now > 0:
                    some(A, 2 * order(A, now, groups), 2, C, range(now), s_a, 5)

        m = j - 1

        @pl.when(has_b & (j > 0) & (j < groups - 1))
        def _():
            send(B, 2 * m).wait_recv()
            send(B, 2 * m + 1).wait_recv()

            @pl.when(even)
            def _():
                whole(B, 2 * order(B, m, groups), 2, C, s_b, 4)

            for now in range(groups - 2):
                @pl.when(has_a & (m == now))
                def _():
                    some(B, 2 * order(B, now, groups), 2, A, range(min(now + 2, groups - now)), s_b, 3)

        return 0

    lax.fori_loop(0, groups, step, 0)

    def message(which, target):
        return pltpu.make_async_remote_copy(
            src_ref=msg.at[which], dst_ref=got.at[which], send_sem=msg_send.at[which],
            recv_sem=msg_recv.at[which], device_id=target, device_id_type=MESH)

    def masked(slot, tile, cluster, values):
        return jnp.where(row(slot, tile) == cluster, jnp.max(values, axis=0, keepdims=True), -1.0)

    def message_a(tile):
        msg[0, pl.ds(tile, 1), :] = jnp.maximum(
            jnp.maximum(masked(A, tile, s_a, pres[0, :, part(tile)]), masked(A, tile, s_b, qacc[3, :, part(tile)])),
            jnp.where(odd, masked(A, tile, s_c, qacc[4, :, part(tile)]), -1.0))

    def message_b(tile):
        msg[1, pl.ds(tile, 1), :] = masked(B, tile, s_b, pres[1, :, part(tile)])

    for tile in range(chunks):
        msg[2, tile:tile + 1, :] = jnp.maximum(
            masked(C, tile, s_c, pres[2, :, part(tile)]), jnp.where(odd, masked(C, tile, s_a, qacc[5, :, part(tile)]), -1.0))

    @pl.when(odd & has_c)
    def _():
        message(2, above).start()

    for tile in range(chunks):
        own = jnp.max(qacc[0, :, part(tile)], axis=0, keepdims=True)
        out_ref[tile:tile + 1, :] = jnp.maximum(
            jnp.maximum(own, -1.0),
            jnp.maximum(masked(OWN, tile, s_a, qacc[1, :, part(tile)]), masked(OWN, tile, s_c, qacc[2, :, part(tile)])))

    @pl.when(edge)
    def _():
        for each in edge_copies():
            each.wait_recv()
        cluster = edge_tags[0:1, 0:1]
        s = lax.dot_general(
            edge_rows[...], blk[OWN, part(0), :], (((1,), (1,)), ((), ())), preferred_element_type=jnp.float32)
        p_bias = columns(jnp.where(edge_tags[chunks:chunks + 1, :] == cluster, 0.0, OUT))
        q_bias = jnp.where(row(OWN, chunks) == cluster, 0.0, OUT)
        rows_best = jnp.max((s + q_bias).T, axis=0, keepdims=True)
        edge_out[...] = jnp.broadcast_to(jnp.where(edge_tags[0:1, :] == cluster, rows_best, -1.0), edge_out.shape)
        edge_message().start()
        own_best = jnp.max(s + p_bias, axis=0, keepdims=True)
        out_ref[0:1, :] = jnp.maximum(out_ref[0:1, :], jnp.where(row(OWN, 0) == cluster, own_best, -1.0))

    @pl.when(has_a & has_b)
    def _():
        some(B, 2 * order(B, 0, groups), 2, A, range(2, groups), s_b, 3)

    for t in range(4, chunks):
        message_a(order(A, t, chunks))
    for t in range(chunks - 4):
        message_b(order(B, t, chunks))

    @pl.when(over_l)
    def _():
        for t in range(chunks - 2, chunks):
            send(B, t).wait_recv()
        some(B, 2 * order(B, groups - 1, groups), 2, A, range(1), s_b, 3)
        for t in range(chunks - 2, chunks):
            message_b(order(B, t, chunks))

    @pl.when(has_b)
    def _():
        m = groups - 2
        send(B, 2 * m).wait_recv()
        send(B, 2 * m + 1).wait_recv()

        @pl.when(has_a)
        def _():
            some(B, 2 * order(B, m, groups), 2, A, range(groups - m), s_b, 3)

        @pl.when(even)
        def _():
            whole(B, 2 * order(B, m, groups), 2, C, s_b, 4)

    for t in range(chunks - 4, chunks - 2):
        message_b(order(B, t, chunks))

    @pl.when(over_l)
    def _():
        message(1, first).start()

    for t in range(2, 4):
        message_a(order(A, t, chunks))

    def last_step(i, _):
        t = i + up_r.astype(jnp.int32) * (2 * chunks - 3 - 2 * i)

        comes = has_b & jnp.logical_not(over_l)

        @pl.when(comes)
        def _():
            send(B, t).wait_recv()

        @pl.when(has_a & comes)
        def _():
            some(B, order(B, t, chunks), 1, A, range(1), s_b, 3)

        @pl.when(odd & comes)
        def _():
            message_b(order(B, t, chunks))

        @pl.when(odd & comes & (i == chunks - 1))
        def _():
            message(1, first).start()

        @pl.when(i == jnp.where(up_l, chunks - 2, chunks - 1))
        def _():
            for each in range(2):
                message_a(order(A, each, chunks))

            @pl.when(up_l)
            def _():
                edge_message().wait_recv()
                msg[0, 0:1, :] = jnp.maximum(msg[0, 0:1, :], edge_got[0:1, :])

            @pl.when(has_a)
            def _():
                message(0, second).start()

        @pl.when(even & has_b)
        def _():
            whole(B, order(B, t, chunks), 1, C, s_b, 4)

        @pl.when(even & has_b)
        def _():
            message_b(order(B, t, chunks))

        return 0

    lax.fori_loop(chunks - 2, chunks, last_step, 0)

    @pl.when(even & has_b)
    def _():
        message(1, first).start()

    @pl.when(even)
    def _():
        for tile in range(chunks):
            msg[2, tile:tile + 1, :] = jnp.maximum(
                msg[2, tile:tile + 1, :], masked(C, tile, s_b, qacc[4, :, part(tile)]))
        message(2, above).start()

    messages = ((has_a, second, has_first), (has_b, first, has_second), (has_c, above, odd | has_down))
    @pl.when(has_first)
    def _():
        for t in range(LEAD + MORE, chunks):
            send(A, t).wait_send()

    @pl.when(has_first & jnp.logical_not(is_r & odd))
    def _():
        for t in range(LEAD, LEAD + MORE):
            send(A, t).wait_send()

    @pl.when(has_second)
    def _():
        for t in range(chunks - DOWN):
            send(B, t).wait_send()

    @pl.when(has_second & jnp.logical_not(over_r))
    def _():
        for t in range(chunks - DOWN, chunks - UP):
            send(B, t).wait_send()

    @pl.when(has_second & jnp.logical_not(over_r | up_l))
    def _():
        for t in range(chunks - UP, chunks):
            send(B, t).wait_send()

    @pl.when(over_r)
    def _():
        for t in range(DOWN):
            over(DOWN, crossing, t, (OWN, relay), over_target).wait_send()

    @pl.when(over_next)
    def _():
        for t in range(DOWN):
            over(DOWN, 0, t, (relay, relay), over_target).wait_send()

    @pl.when(over_y)
    def _():
        for i in range(crossings):
            for t in range(DOWN):
                over(DOWN, i, t, (relay, B), l_at(i)).wait_send()

    @pl.when(up_l)
    def _():
        for t in range(UP):
            over(UP, crossing, t, (OWN, relay), over_target).wait_send()

    @pl.when(up_pass)
    def _():
        for t in range(UP):
            over(UP, 2, t, (relay, relay), over_target).wait_send()

    @pl.when(up_mid)
    def _():
        for t in range(UP):
            over(UP, 1, t, (relay, B), r_at(1)).wait_send()

    @pl.when(up_y)
    def _():
        for i in range(crossings):
            for t in range(UP):
                over(UP, i, t, (relay, relay if i == 1 else B), r_at(0 if i == 1 else i)).wait_send()

    @pl.when(gives_c)
    def _():
        for t in range(chunks):
            send(C, t).wait_send()

    @pl.when(up_l)
    def _():
        for each in edge_copies():
            each.wait_send()

    @pl.when(edge)
    def _():
        edge_message().wait_send()

    for which, (gives, target, gets) in enumerate(messages):
        @pl.when(gives)
        def _():
            message(which, target).wait_send()

        @pl.when(gets)
        def _():
            message(which, target).wait_recv()
            out_ref[...] = jnp.maximum(out_ref[...], got[which])


def shards(n_slab, n_member, embeddings, cluster_ids, keep_mask):
    rows, width = embeddings.shape
    chunks = rows // LANES
    crossings = n_slab * n_member // 2 // PLANE - 1
    highest = pl.pallas_call(
        functools.partial(kernel, n_slab, n_member),
        out_shape=jax.ShapeDtypeStruct((chunks, LANES), jnp.float32),
        in_specs=[pl.BlockSpec(memory_space=pltpu.HBM)] * 3,
        out_specs=pl.BlockSpec(memory_space=pltpu.VMEM),
        scratch_shapes=[
            pltpu.VMEM((rows, width), jnp.bfloat16),
            pltpu.VMEM((4, rows, width), jnp.bfloat16),
            pltpu.VMEM((4, 2 * chunks, LANES), jnp.int32),
            pltpu.VMEM((3, 8, rows), jnp.float32),
            pltpu.VMEM((6, 8, rows), jnp.float32),
            pltpu.VMEM((3, chunks, LANES), jnp.float32),
            pltpu.VMEM((3, chunks, LANES), jnp.float32),
            pltpu.VMEM((crossings, DOWN, LANES, width), jnp.bfloat16),
            pltpu.SemaphoreType.DMA((chunks + 2,)),
            pltpu.SemaphoreType.DMA((4, chunks)),
            pltpu.SemaphoreType.DMA((4, chunks)),
            pltpu.SemaphoreType.DMA((4,)),
            pltpu.SemaphoreType.DMA((4,)),
            pltpu.SemaphoreType.DMA((3,)),
            pltpu.SemaphoreType.DMA((3,)),
            pltpu.SemaphoreType.DMA((crossings, DOWN)),
            pltpu.SemaphoreType.DMA((crossings, DOWN)),
            pltpu.SemaphoreType.REGULAR,
            pltpu.SemaphoreType.REGULAR,
            pltpu.VMEM((LANES, width), jnp.bfloat16),
            pltpu.VMEM((2 * chunks, LANES), jnp.int32),
            pltpu.VMEM((8, LANES), jnp.float32),
            pltpu.VMEM((8, LANES), jnp.float32),
            pltpu.SemaphoreType.DMA((3,)),
            pltpu.SemaphoreType.DMA((3,)),
        ],
        compiler_params=pltpu.CompilerParams(
            collective_id=0, has_side_effects=True, vmem_limit_bytes=40 << 20),
    )(*(pltpu.with_memory_space_constraint(each, pltpu.HBM) for each in (
        embeddings, cluster_ids.reshape(chunks, LANES), keep_mask.reshape(chunks, LANES))))
    return highest.reshape(rows)


def solution(mesh):
    placed = (P(("slab", "member"), None), P(("slab", "member")), P(("slab", "member")))
    return jax.shard_map(
        functools.partial(shards, mesh.shape["slab"], mesh.shape["member"]),
        mesh=mesh, in_specs=placed, out_specs=P(("slab", "member")), check_vma=False,
    )
```

```python
import functools

import jax
import jax.numpy as jnp
from jax import lax
from jax.experimental import pallas as pl
from jax.experimental.pallas import tpu as pltpu
from jax.sharding import PartitionSpec as P

MESH = pl.DeviceIdType.MESH
OWN, A, B, C = 0, 1, 2, 3
LANES = 128
GROUP = 2 * LANES
LEAD = 5
MORE = 2
PLANE = 16
DOWN, UP = 3, 1
OUT = -4.0


def kernel(n_slab, n_member, x_ref, ids_ref, keep_ref, out_ref, raw, blk, tags, pres, qacc, msg, got,
           relay, load_sem, send_sem, recv_sem, tag_send, tag_recv, msg_send, msg_recv, over_send, over_recv, ready, early,
           edge_rows, edge_tags, edge_out, edge_got, edge_send, edge_recv):
    rows, width = raw.shape
    chunks, groups = rows // LANES, rows // GROUP
    count = n_slab * n_member
    slab, member = lax.axis_index("slab"), lax.axis_index("member")
    core = lax.rem(member, 2)
    place = slab * n_member + member
    chip = lax.div(place, 2)
    has_down, has_up = chip > 0, chip < count // 2 - 1
    even, odd = core == 0, core == 1

    def device(at):
        at = jnp.clip(at, 0, count - 1)
        return (lax.div(at, n_member), lax.rem(at, n_member))

    first, second = device(place - 2 + 4 * core), device(place + 2 - 4 * core)
    has_first = (even & has_down) | (odd & has_up)
    has_second = (even & has_up) | (odd & has_down)
    has_a, has_b, has_c = has_second, has_first, even | has_up
    gives_c = odd | has_up
    step_at = lax.rem(chip, PLANE)
    over_r, over_l = odd & (step_at == 0) & has_down, odd & (step_at == PLANE - 1) & has_up
    over_y = odd & (chip == count // 2 - 1)
    crossings = count // 2 // PLANE - 1
    crossing = lax.div(chip + 1, PLANE) - 1
    is_r, above_r = (step_at == 0) & has_down, (step_at == 1) & (chip > PLANE)
    over_first, over_next = over_r & (crossing == 0), over_r & (crossing == 1)
    over_to_y = over_r & jnp.logical_not(over_first)
    up_r, up_l = even & (step_at == 0) & has_down, even & (step_at == PLANE - 1) & has_up
    up_y = even & (chip == 0)
    up_mid, up_far = up_r & (crossing == 0), up_r & (crossing == 1)
    edge = even & (step_at == PLANE - 2) & (chip < count // 2 - PLANE)
    up_last, up_pass = up_l & (crossing == 2), up_l & (crossing == 1)
    c_source = jnp.where(even, A, OWN)
    sibling = (slab, member + 1 - 2 * core)
    above, below = device(place + 1), device(place - 1)

    barrier = pltpu.get_barrier_semaphore()
    partners = ((has_first, first), (has_second, second), (place < count - 1, above), (place > 0, below))
    told = partners + ((over_to_y | over_l, device(count - 1)), (over_next | up_far, device(place - 2 * PLANE)), (up_r & jnp.logical_not(up_far), device(0)))
    told = told + ((up_pass, device(place + 2 * PLANE)),)
    told = told + tuple((up_y, device(2 * (PLANE * (i + 1) - 1))) for i in range(crossings - 1))
    for there, other in told[:2]:
        @pl.when(there & jnp.logical_not(above_r & (odd if other is second else even)))
        def _():
            pl.semaphore_signal(barrier, inc=1, device_id=other, device_id_type=MESH)

    for there, other in told[2:]:
        @pl.when(there)
        def _():
            pl.semaphore_signal(barrier, inc=1, device_id=other, device_id_type=MESH)

    def part(t):
        return pl.ds(pl.multiple_of(t * LANES, LANES), LANES)

    def group_at(g):
        return pl.ds(pl.multiple_of(g * GROUP, GROUP), GROUP)

    def order(slot, t, count):
        if slot == C:
            return t
        flip = core if slot == A else 1 - core
        return t + flip * (count - 1 - 2 * t)

    def load(t):
        return pltpu.make_async_copy(x_ref.at[part(t)], raw.at[part(t)], load_sem.at[t])

    def send(slot, t):
        source, target = {A: (OWN, first), B: (OWN, second), C: (c_source, sibling)}[slot]
        rows_of = part(order(slot, t, chunks))
        return pltpu.make_async_remote_copy(
            src_ref=blk.at[source, rows_of], dst_ref=blk.at[slot, rows_of],
            send_sem=send_sem.at[slot, t], recv_sem=recv_sem.at[slot, t],
            device_id=target, device_id_type=MESH)

    def send_tags(src_slot, dst_slot, target):
        return pltpu.make_async_remote_copy(
            src_ref=tags.at[src_slot], dst_ref=tags.at[dst_slot], send_sem=tag_send.at[dst_slot],
            recv_sem=tag_recv.at[dst_slot], device_id=target, device_id_type=MESH)

    load_ids = pltpu.make_async_copy(ids_ref, tags.at[OWN, 0:chunks], load_sem.at[chunks])
    load_keep = pltpu.make_async_copy(keep_ref, tags.at[OWN, chunks:2 * chunks], load_sem.at[chunks + 1])
    load(order(A, 0, chunks)).start()
    load_ids.start()
    load_keep.start()
    for t in range(1, chunks):
        load(order(A, t, chunks)).start()
    for slot, there in ((A, has_a), (B, has_b), (C, has_c)):
        @pl.when(jnp.logical_not(there))
        def _():
            tags[slot] = jnp.full(tags.shape[1:], -2, jnp.int32)

    def normalise(t):
        load(t).wait()
        values = raw[part(t), :].astype(jnp.float32)
        scale = lax.rsqrt(jnp.sum(values * values, axis=1, keepdims=True) + 1e-06)
        blk[OWN, part(t), :] = (values * scale).astype(jnp.bfloat16)

    normalise(order(A, 0, chunks))
    load_ids.wait()
    load_keep.wait()
    tags[OWN, chunks:2 * chunks] = jnp.where(tags[OWN, chunks:2 * chunks] == 1, tags[OWN, 0:chunks], -1)
    heard = sum(there.astype(jnp.int32) for there, _ in partners)
    heard = heard + over_first.astype(jnp.int32) + over_y.astype(jnp.int32) * (2 * crossings - 1)
    heard = heard + (up_l | up_mid).astype(jnp.int32) + up_y.astype(jnp.int32) * (crossings - 1)
    heard = heard - is_r.astype(jnp.int32)

    @pl.when(jnp.logical_not(is_r))
    def _():
        pl.semaphore_wait(barrier, heard)

    @pl.when(above_r)
    def _():
        pl.semaphore_signal(early, inc=1, device_id=device(place - 2), device_id_type=MESH)

    @pl.when(is_r)
    def _():
        pl.semaphore_wait(early, 1)

    @pl.when(over_y)
    def _():
        for i in range(1, crossings):
            pl.semaphore_signal(ready, inc=1, device_id=device(2 * PLANE * (i + 1) + 1), device_id_type=MESH)

    first_now, second_now = has_first & jnp.logical_not(is_r & even), has_second & jnp.logical_not(is_r & odd)

    @pl.when(first_now)
    def _():
        send(A, 0).start()
        send_tags(OWN, A, first).start()

    @pl.when(second_now)
    def _():
        send_tags(OWN, B, second).start()

    def prepare(t, _):
        normalise(order(A, t, chunks))

        @pl.when(first_now)
        def _():
            send(A, t).start()

        return 0

    lax.fori_loop(1, chunks, prepare, 0)

    @pl.when(odd & jnp.logical_not(is_r))
    def _():
        for t in range(chunks):
            send(C, t).start()

    pres[...] = jnp.full(pres.shape, OUT, jnp.float32)
    qacc[...] = jnp.full(qacc.shape, OUT, jnp.float32)

    def row(slot, t):
        return tags[slot, pl.ds(t, 1), :]

    def columns(values):
        return jnp.broadcast_to(values, (LANES, LANES)).T

    def fold(values):
        return jnp.max(values.reshape(values.shape[0] // 8, 8, LANES), axis=0)

    def scores(p, q_slot, g):
        q = blk[q_slot, group_at(g), :]
        return lax.dot_general(p, q, (((1,), (1,)), ((), ())), preferred_element_type=jnp.float32)

    def own_step(t, _):
        p = blk[OWN, group_at(t), :]
        labels = jnp.concatenate(
            [columns(row(OWN, chunks + 2 * t + i).astype(jnp.float32)) for i in range(2)], axis=0)
        down = lax.broadcasted_iota(jnp.int32, (2 * LANES, LANES), 0) + t * 2 * LANES
        along = lax.broadcasted_iota(jnp.int32, (2 * LANES, LANES), 1)
        for n in range(chunks // 2):
            s = scores(p, OWN, n)
            for h in range(2):
                tile = 2 * n + h
                ids = row(OWN, tile).astype(jnp.float32)
                hits = (labels == ids) & (down != along + tile * LANES)
                top = fold(jnp.where(hits, s[:, h * LANES:(h + 1) * LANES], OUT))
                at = (0, slice(None), slice(tile * LANES, (tile + 1) * LANES))
                qacc[at] = jnp.maximum(qacc[at], top)
        return 0

    def shared(slot):
        low, high = tags[slot, 0:1, 0:1], tags[slot, chunks - 1:chunks, LANES - 1:LANES]
        if slot == C:
            return low
        return jnp.where(core == (0 if slot == A else 1), low, high)

    def biases(p_slot, t, size, cluster):
        each = [columns(jnp.where(row(p_slot, chunks + t + i) == cluster, 0.0, OUT)) for i in range(size)]
        return jnp.concatenate(each, axis=0) if size > 1 else each[0]

    def tile_pair(p, p_bias, best, q_slot, g, cluster, q_at):
        s = scores(p, q_slot, g)
        for h in range(2):
            one = s[:, h * LANES:(h + 1) * LANES]
            q_bias = jnp.where(row(q_slot, chunks + 2 * g + h) == cluster, 0.0, OUT)
            best = jnp.maximum(best, one + q_bias)
            at = (q_at, slice(None), part(2 * g + h))
            qacc[at] = jnp.maximum(qacc[at], fold(one + p_bias))
        return best

    def keep_rows(p_slot, t, size, best):
        for i in range(size):
            at = (p_slot - 1, slice(None), part(t + i))
            pres[at] = jnp.maximum(pres[at], fold(best[i * LANES:(i + 1) * LANES].T))

    def whole(p_slot, t, size, q_slot, cluster, q_at):
        p = blk[p_slot, pl.ds(pl.multiple_of(t * LANES, LANES), size * LANES), :]
        p_bias = biases(p_slot, t, size, cluster)
        best = jnp.full((size * LANES, LANES), OUT, jnp.float32)
        for g in range(groups):
            best = tile_pair(p, p_bias, best, q_slot, g, cluster, q_at)
        keep_rows(p_slot, t, size, best)

    def some(p_slot, t, size, q_slot, arrivals, cluster, q_at):
        p = blk[p_slot, pl.ds(pl.multiple_of(t * LANES, LANES), size * LANES), :]
        p_bias = biases(p_slot, t, size, cluster)
        best = jnp.full((size * LANES, LANES), OUT, jnp.float32)
        for i in arrivals:
            best = tile_pair(p, p_bias, best, q_slot, order(q_slot, i, groups), cluster, q_at)
        keep_rows(p_slot, t, size, best)

    over_target = device(jnp.where(even, jnp.where(up_last, place - 2 * PLANE, 0), jnp.where(crossing == 0, place + 2 * PLANE, count - 1)))

    def l_at(i):
        return device(2 * (PLANE * (i + 1) - 1) + core)

    def r_at(i):
        return device(2 * PLANE * (i + 1) + core)

    def over(total, i, t, way, target):
        source, there = way
        rows_of = part(order(B, chunks - total + t, chunks))
        return pltpu.make_async_remote_copy(
            src_ref=relay.at[i, t] if source is relay else blk.at[OWN, rows_of],
            dst_ref=relay.at[i, t] if there is relay else blk.at[B, rows_of],
            send_sem=over_send.at[i, t],
            recv_sem=over_recv.at[i, t] if there is relay else recv_sem.at[B, chunks - total + t],
            device_id=target, device_id_type=MESH)

    @pl.when(up_l)
    def _():
        for t in range(UP):
            over(UP, crossing, t, (OWN, relay), over_target).start()

    @pl.when(is_r)
    def _():
        pl.semaphore_wait(barrier, heard)

    @pl.when(is_r & even)
    def _():
        send_tags(OWN, A, first).start()
        for t in range(chunks):
            send(A, t).start()

    @pl.when(is_r & odd)
    def _():
        send_tags(OWN, B, second).start()
        for t in range(chunks):
            send(C, t).start()

    @pl.when(over_first)
    def _():
        for t in range(DOWN):
            over(DOWN, crossing, t, (OWN, relay), over_target).start()


    lax.fori_loop(0, groups, own_step, 0)

    @pl.when(over_to_y)
    def _():
        pl.semaphore_wait(ready, 1)
        for t in range(DOWN):
            over(DOWN, crossing, t, (OWN, relay), over_target).start()

    @pl.when(up_pass)
    def _():
        for t in range(UP):
            over(UP, 2, t, (OWN, relay), first).wait_recv()
            over(UP, 2, t, (relay, relay), over_target).start()

    @pl.when(over_next)
    def _():
        for t in range(DOWN):
            over(DOWN, 0, t, (OWN, relay), first).wait_recv()
            over(DOWN, 0, t, (relay, relay), over_target).start()

    @pl.when(has_first)
    def _():
        for t in range(LEAD):
            send(A, t).wait_send()

    @pl.when(is_r & odd)
    def _():
        for t in range(LEAD, LEAD + MORE):
            send(A, t).wait_send()

    @pl.when(has_second)
    def _():
        for t in range(chunks - DOWN):
            send(B, t).start()

    @pl.when(has_second & jnp.logical_not(over_r))
    def _():
        for t in range(chunks - DOWN, chunks - UP):
            send(B, t).start()

    @pl.when(has_second & jnp.logical_not(over_r | up_l))
    def _():
        for t in range(chunks - UP, chunks):
            send(B, t).start()

    @pl.when(has_first)
    def _():
        send_tags(OWN, A, first).wait_send()

    @pl.when(has_second)
    def _():
        send_tags(OWN, B, second).wait_send()

    @pl.when(has_a)
    def _():
        send_tags(OWN, A, first).wait_recv()

    @pl.when(has_b)
    def _():
        send_tags(OWN, B, second).wait_recv()

    @pl.when(gives_c)
    def _():
        send_tags(c_source, C, sibling).start()
        send_tags(c_source, C, sibling).wait_send()

    @pl.when(has_c)
    def _():
        send_tags(c_source, C, sibling).wait_recv()

    s_a, s_b, s_c = shared(A), shared(B), shared(C)

    @pl.when(even)
    def _():
        for t in range(chunks):
            send(C, t).wait_recv()

    def edge_copies():
        return (
            pltpu.make_async_remote_copy(
                src_ref=blk.at[A, part(0)], dst_ref=edge_rows, send_sem=edge_send.at[0], recv_sem=edge_recv.at[0],
                device_id=first, device_id_type=MESH),
            pltpu.make_async_remote_copy(
                src_ref=tags.at[A], dst_ref=edge_tags, send_sem=edge_send.at[1], recv_sem=edge_recv.at[1],
                device_id=first, device_id_type=MESH))

    def edge_message():
        return pltpu.make_async_remote_copy(
            src_ref=edge_out, dst_ref=edge_got, send_sem=edge_send.at[2], recv_sem=edge_recv.at[2],
            device_id=second, device_id_type=MESH)

    def step(j, _):
        @pl.when(up_mid & (j == groups - 1))
        def _():
            for t in range(UP):
                over(UP, 1, t, (OWN, relay), first).wait_recv()
                over(UP, 1, t, (relay, B), r_at(1)).start()

        @pl.when(over_y & (j == groups - 3))
        def _():
            for i in range(crossings):
                for t in range(DOWN):
                    over(DOWN, i, t, (OWN, relay), first).wait_recv()
                    over(DOWN, i, t, (relay, B), l_at(i)).start()

        @pl.when(up_y & (j == groups - 2))
        def _():
            for i in (1, 0, 2):
                for t in range(UP):
                    over(UP, i, t, (OWN, relay), first).wait_recv()
                    over(UP, i, t, (relay, relay if i == 1 else B), r_at(0 if i == 1 else i)).start()

        @pl.when(has_a)
        def _():
            send(A, 2 * j).wait_recv()
            send(A, 2 * j + 1).wait_recv()

        @pl.when(even & has_a)
        def _():
            send(C, 2 * j).start()
            send(C, 2 * j + 1).start()

        @pl.when(up_l & (j == 0))
        def _():
            for each in edge_copies():
                each.start()

        @pl.when(has_a)
        def _():
            whole(A, 2 * order(A, j, groups), 2, OWN, s_a, 1)

        @pl.when(odd & has_c)
        def _():
            send(C, 2 * j).wait_recv()
            send(C, 2 * j + 1).wait_recv()

        @pl.when(has_c)
        def _():
            whole(C, 2 * j, 2, OWN, s_c, 2)

        for now in range(groups):
            @pl.when(odd & has_a & has_c & (j == now))
            def _():
                some(C, 2 * now, 2, A, range(now + 1), s_c, 4)
                if now > 0:
                    some(A, 2 * order(A, now, groups), 2, C, range(now), s_a, 5)

        m = j - 1

        @pl.when(has_b & (j > 0) & (j < groups - 1))
        def _():
            send(B, 2 * m).wait_recv()
            send(B, 2 * m + 1).wait_recv()

            @pl.when(even)
            def _():
                whole(B, 2 * order(B, m, groups), 2, C, s_b, 4)

            for now in range(groups - 2):
                @pl.when(has_a & (m == now))
                def _():
                    some(B, 2 * order(B, now, groups), 2, A, range(min(now + 2, groups - now)), s_b, 3)

        return 0

    lax.fori_loop(0, groups, step, 0)

    def message(which, target):
        return pltpu.make_async_remote_copy(
            src_ref=msg.at[which], dst_ref=got.at[which], send_sem=msg_send.at[which],
            recv_sem=msg_recv.at[which], device_id=target, device_id_type=MESH)

    def masked(slot, tile, cluster, values):
        return jnp.where(row(slot, tile) == cluster, jnp.max(values, axis=0, keepdims=True), -1.0)

    def message_a(tile):
        msg[0, pl.ds(tile, 1), :] = jnp.maximum(
            jnp.maximum(masked(A, tile, s_a, pres[0, :, part(tile)]), masked(A, tile, s_b, qacc[3, :, part(tile)])),
            jnp.where(odd, masked(A, tile, s_c, qacc[4, :, part(tile)]), -1.0))

    def message_b(tile):
        msg[1, pl.ds(tile, 1), :] = masked(B, tile, s_b, pres[1, :, part(tile)])

    for tile in range(chunks):
        msg[2, tile:tile + 1, :] = jnp.maximum(
            masked(C, tile, s_c, pres[2, :, part(tile)]), jnp.where(odd, masked(C, tile, s_a, qacc[5, :, part(tile)]), -1.0))

    @pl.when(odd & has_c)
    def _():
        message(2, above).start()

    for tile in range(chunks):
        own = jnp.max(qacc[0, :, part(tile)], axis=0, keepdims=True)
        out_ref[tile:tile + 1, :] = jnp.maximum(
            jnp.maximum(own, -1.0),
            jnp.maximum(masked(OWN, tile, s_a, qacc[1, :, part(tile)]), masked(OWN, tile, s_c, qacc[2, :, part(tile)])))

    @pl.when(edge)
    def _():
        for each in edge_copies():
            each.wait_recv()
        cluster = edge_tags[0:1, 0:1]
        s = lax.dot_general(
            edge_rows[...], blk[OWN, part(0), :], (((1,), (1,)), ((), ())), preferred_element_type=jnp.float32)
        p_bias = columns(jnp.where(edge_tags[chunks:chunks + 1, :] == cluster, 0.0, OUT))
        q_bias = jnp.where(row(OWN, chunks) == cluster, 0.0, OUT)
        rows_best = jnp.max((s + q_bias).T, axis=0, keepdims=True)
        edge_out[...] = jnp.broadcast_to(jnp.where(edge_tags[0:1, :] == cluster, rows_best, -1.0), edge_out.shape)
        edge_message().start()
        own_best = jnp.max(s + p_bias, axis=0, keepdims=True)
        out_ref[0:1, :] = jnp.maximum(out_ref[0:1, :], jnp.where(row(OWN, 0) == cluster, own_best, -1.0))

    @pl.when(has_a & has_b)
    def _():
        some(B, 2 * order(B, 0, groups), 2, A, range(2, groups), s_b, 3)

    for t in range(4, chunks):
        message_a(order(A, t, chunks))
    for t in range(chunks - 4):
        message_b(order(B, t, chunks))

    @pl.when(over_l)
    def _():
        for t in range(chunks - 2, chunks):
            send(B, t).wait_recv()
        some(B, 2 * order(B, groups - 1, groups), 2, A, range(1), s_b, 3)
        for t in range(chunks - 2, chunks):
            message_b(order(B, t, chunks))

    @pl.when(has_b)
    def _():
        m = groups - 2
        send(B, 2 * m).wait_recv()
        send(B, 2 * m + 1).wait_recv()

        @pl.when(has_a)
        def _():
            some(B, 2 * order(B, m, groups), 2, A, range(groups - m), s_b, 3)

        @pl.when(even & jnp.logical_not(up_l))
        def _():
            whole(B, 2 * order(B, m, groups), 2, C, s_b, 4)

    for t in range(chunks - 4, chunks - 2):
        message_b(order(B, t, chunks))

    @pl.when(over_l)
    def _():
        message(1, first).start()

    for t in range(2, 4):
        message_a(order(A, t, chunks))

    def last_step(i, _):
        t = i + up_r.astype(jnp.int32) * (2 * chunks - 3 - 2 * i)

        comes = has_b & jnp.logical_not(over_l)

        @pl.when(comes)
        def _():
            send(B, t).wait_recv()

        @pl.when(has_a & comes)
        def _():
            some(B, order(B, t, chunks), 1, A, range(1), s_b, 3)

        @pl.when(odd & comes)
        def _():
            message_b(order(B, t, chunks))

        @pl.when(odd & comes & (i == chunks - 1))
        def _():
            message(1, first).start()

        @pl.when(i == jnp.where(up_l, chunks - 2, chunks - 1))
        def _():
            for each in range(2):
                message_a(order(A, each, chunks))

            @pl.when(up_l)
            def _():
                edge_message().wait_recv()
                msg[0, 0:1, :] = jnp.maximum(msg[0, 0:1, :], edge_got[0:1, :])

            @pl.when(has_a)
            def _():
                message(0, second).start()

            @pl.when(up_l)
            def _():
                whole(B, 2 * order(B, groups - 2, groups), 2, C, s_b, 4)
                for each in range(chunks - 4, chunks - 2):
                    message_b(order(B, each, chunks))

        @pl.when(even & has_b)
        def _():
            whole(B, order(B, t, chunks), 1, C, s_b, 4)

        @pl.when(even & has_b)
        def _():
            message_b(order(B, t, chunks))

        return 0

    lax.fori_loop(chunks - 2, chunks, last_step, 0)

    @pl.when(even & has_b)
    def _():
        message(1, first).start()

    @pl.when(even)
    def _():
        for tile in range(chunks):
            msg[2, tile:tile + 1, :] = jnp.maximum(
                msg[2, tile:tile + 1, :], masked(C, tile, s_b, qacc[4, :, part(tile)]))
        message(2, above).start()

    messages = ((has_a, second, has_first), (has_b, first, has_second), (has_c, above, odd | has_down))
    @pl.when(has_first)
    def _():
        for t in range(LEAD + MORE, chunks):
            send(A, t).wait_send()

    @pl.when(has_first & jnp.logical_not(is_r & odd))
    def _():
        for t in range(LEAD, LEAD + MORE):
            send(A, t).wait_send()

    @pl.when(has_second)
    def _():
        for t in range(chunks - DOWN):
            send(B, t).wait_send()

    @pl.when(has_second & jnp.logical_not(over_r))
    def _():
        for t in range(chunks - DOWN, chunks - UP):
            send(B, t).wait_send()

    @pl.when(has_second & jnp.logical_not(over_r | up_l))
    def _():
        for t in range(chunks - UP, chunks):
            send(B, t).wait_send()

    @pl.when(over_r)
    def _():
        for t in range(DOWN):
            over(DOWN, crossing, t, (OWN, relay), over_target).wait_send()

    @pl.when(over_next)
    def _():
        for t in range(DOWN):
            over(DOWN, 0, t, (relay, relay), over_target).wait_send()

    @pl.when(over_y)
    def _():
        for i in range(crossings):
            for t in range(DOWN):
                over(DOWN, i, t, (relay, B), l_at(i)).wait_send()

    @pl.when(up_l)
    def _():
        for t in range(UP):
            over(UP, crossing, t, (OWN, relay), over_target).wait_send()

    @pl.when(up_pass)
    def _():
        for t in range(UP):
            over(UP, 2, t, (relay, relay), over_target).wait_send()

    @pl.when(up_mid)
    def _():
        for t in range(UP):
            over(UP, 1, t, (relay, B), r_at(1)).wait_send()

    @pl.when(up_y)
    def _():
        for i in range(crossings):
            for t in range(UP):
                over(UP, i, t, (relay, relay if i == 1 else B), r_at(0 if i == 1 else i)).wait_send()

    @pl.when(gives_c)
    def _():
        for t in range(chunks):
            send(C, t).wait_send()

    @pl.when(up_l)
    def _():
        for each in edge_copies():
            each.wait_send()

    @pl.when(edge)
    def _():
        edge_message().wait_send()

    for which, (gives, target, gets) in enumerate(messages):
        @pl.when(gives)
        def _():
            message(which, target).wait_send()

        @pl.when(gets)
        def _():
            message(which, target).wait_recv()
            out_ref[...] = jnp.maximum(out_ref[...], got[which])


def shards(n_slab, n_member, embeddings, cluster_ids, keep_mask):
    rows, width = embeddings.shape
    chunks = rows // LANES
    crossings = n_slab * n_member // 2 // PLANE - 1
    highest = pl.pallas_call(
        functools.partial(kernel, n_slab, n_member),
        out_shape=jax.ShapeDtypeStruct((chunks, LANES), jnp.float32),
        in_specs=[pl.BlockSpec(memory_space=pltpu.HBM)] * 3,
        out_specs=pl.BlockSpec(memory_space=pltpu.VMEM),
        scratch_shapes=[
            pltpu.VMEM((rows, width), jnp.bfloat16),
            pltpu.VMEM((4, rows, width), jnp.bfloat16),
            pltpu.VMEM((4, 2 * chunks, LANES), jnp.int32),
            pltpu.VMEM((3, 8, rows), jnp.float32),
            pltpu.VMEM((6, 8, rows), jnp.float32),
            pltpu.VMEM((3, chunks, LANES), jnp.float32),
            pltpu.VMEM((3, chunks, LANES), jnp.float32),
            pltpu.VMEM((crossings, DOWN, LANES, width), jnp.bfloat16),
            pltpu.SemaphoreType.DMA((chunks + 2,)),
            pltpu.SemaphoreType.DMA((4, chunks)),
            pltpu.SemaphoreType.DMA((4, chunks)),
            pltpu.SemaphoreType.DMA((4,)),
            pltpu.SemaphoreType.DMA((4,)),
            pltpu.SemaphoreType.DMA((3,)),
            pltpu.SemaphoreType.DMA((3,)),
            pltpu.SemaphoreType.DMA((crossings, DOWN)),
            pltpu.SemaphoreType.DMA((crossings, DOWN)),
            pltpu.SemaphoreType.REGULAR,
            pltpu.SemaphoreType.REGULAR,
            pltpu.VMEM((LANES, width), jnp.bfloat16),
            pltpu.VMEM((2 * chunks, LANES), jnp.int32),
            pltpu.VMEM((8, LANES), jnp.float32),
            pltpu.VMEM((8, LANES), jnp.float32),
            pltpu.SemaphoreType.DMA((3,)),
            pltpu.SemaphoreType.DMA((3,)),
        ],
        compiler_params=pltpu.CompilerParams(
            collective_id=0, has_side_effects=True, vmem_limit_bytes=40 << 20),
    )(*(pltpu.with_memory_space_constraint(each, pltpu.HBM) for each in (
        embeddings, cluster_ids.reshape(chunks, LANES), keep_mask.reshape(chunks, LANES))))
    return highest.reshape(rows)


def solution(mesh):
    placed = (P(("slab", "member"), None), P(("slab", "member")), P(("slab", "member")))
    return jax.shard_map(
        functools.partial(shards, mesh.shape["slab"], mesh.shape["member"]),
        mesh=mesh, in_specs=placed, out_specs=P(("slab", "member")), check_vma=False,
    )
```

```python
import functools

import jax
import jax.numpy as jnp
from jax import lax
from jax.experimental import pallas as pl
from jax.experimental.pallas import tpu as pltpu
from jax.sharding import PartitionSpec as P

MESH = pl.DeviceIdType.MESH
OWN, A, B, C = 0, 1, 2, 3
LANES = 128
GROUP = 2 * LANES
LEAD = 5
MORE = 2
PLANE = 16
DOWN, UP = 3, 1
OUT = -4.0


def kernel(n_slab, n_member, x_ref, ids_ref, keep_ref, out_ref, raw, blk, tags, pres, qacc, msg, got,
           relay, load_sem, send_sem, recv_sem, tag_send, tag_recv, msg_send, msg_recv, over_send, over_recv, ready, early,
           edge_rows, edge_tags, edge_out, edge_got, edge_send, edge_recv):
    rows, width = raw.shape
    chunks, groups = rows // LANES, rows // GROUP
    count = n_slab * n_member
    slab, member = lax.axis_index("slab"), lax.axis_index("member")
    core = lax.rem(member, 2)
    place = slab * n_member + member
    chip = lax.div(place, 2)
    has_down, has_up = chip > 0, chip < count // 2 - 1
    even, odd = core == 0, core == 1

    def device(at):
        at = jnp.clip(at, 0, count - 1)
        return (lax.div(at, n_member), lax.rem(at, n_member))

    first, second = device(place - 2 + 4 * core), device(place + 2 - 4 * core)
    has_first = (even & has_down) | (odd & has_up)
    has_second = (even & has_up) | (odd & has_down)
    has_a, has_b, has_c = has_second, has_first, even | has_up
    gives_c = odd | has_up
    step_at = lax.rem(chip, PLANE)
    over_r, over_l = odd & (step_at == 0) & has_down, odd & (step_at == PLANE - 1) & has_up
    over_y = odd & (chip == count // 2 - 1)
    crossings = count // 2 // PLANE - 1
    crossing = lax.div(chip + 1, PLANE) - 1
    is_r, above_r = (step_at == 0) & has_down, (step_at == 1) & (chip > PLANE)
    over_first, over_next = over_r & (crossing == 0), over_r & (crossing == 1)
    over_to_y = over_r & jnp.logical_not(over_first)
    up_r, up_l = even & (step_at == 0) & has_down, even & (step_at == PLANE - 1) & has_up
    up_y = even & (chip == 0)
    up_mid, up_far = up_r & (crossing == 0), up_r & (crossing == 1)
    edge = even & (step_at == PLANE - 2) & (chip < count // 2 - PLANE)
    up_last, up_pass = up_l & (crossing == 2), up_l & (crossing == 1)
    c_source = jnp.where(even, A, OWN)
    sibling = (slab, member + 1 - 2 * core)
    above, below = device(place + 1), device(place - 1)

    barrier = pltpu.get_barrier_semaphore()
    partners = ((has_first, first), (has_second, second), (place < count - 1, above), (place > 0, below))
    told = partners + ((over_to_y | over_l, device(count - 1)), (over_next | up_far, device(place - 2 * PLANE)), (up_r & jnp.logical_not(up_far), device(0)))
    told = told + ((up_pass, device(place + 2 * PLANE)),)
    told = told + tuple((up_y, device(2 * (PLANE * (i + 1) - 1))) for i in range(crossings - 1))
    for there, other in told[:2]:
        @pl.when(there & jnp.logical_not(above_r & (odd if other is second else even)))
        def _():
            pl.semaphore_signal(barrier, inc=1, device_id=other, device_id_type=MESH)

    for there, other in told[2:]:
        @pl.when(there)
        def _():
            pl.semaphore_signal(barrier, inc=1, device_id=other, device_id_type=MESH)

    def part(t):
        return pl.ds(pl.multiple_of(t * LANES, LANES), LANES)

    def group_at(g):
        return pl.ds(pl.multiple_of(g * GROUP, GROUP), GROUP)

    def order(slot, t, count):
        if slot == C:
            return t
        flip = core if slot == A else 1 - core
        return t + flip * (count - 1 - 2 * t)

    def load(t):
        return pltpu.make_async_copy(x_ref.at[part(t)], raw.at[part(t)], load_sem.at[t])

    def send(slot, t):
        source, target = {A: (OWN, first), B: (OWN, second), C: (c_source, sibling)}[slot]
        rows_of = part(order(slot, t, chunks))
        return pltpu.make_async_remote_copy(
            src_ref=blk.at[source, rows_of], dst_ref=blk.at[slot, rows_of],
            send_sem=send_sem.at[slot, t], recv_sem=recv_sem.at[slot, t],
            device_id=target, device_id_type=MESH)

    def send_tags(src_slot, dst_slot, target):
        return pltpu.make_async_remote_copy(
            src_ref=tags.at[src_slot], dst_ref=tags.at[dst_slot], send_sem=tag_send.at[dst_slot],
            recv_sem=tag_recv.at[dst_slot], device_id=target, device_id_type=MESH)

    load_ids = pltpu.make_async_copy(ids_ref, tags.at[OWN, 0:chunks], load_sem.at[chunks])
    load_keep = pltpu.make_async_copy(keep_ref, tags.at[OWN, chunks:2 * chunks], load_sem.at[chunks + 1])
    load(order(A, 0, chunks)).start()
    load_ids.start()
    load_keep.start()
    for t in range(1, chunks):
        load(order(A, t, chunks)).start()
    for slot, there in ((A, has_a), (B, has_b), (C, has_c)):
        @pl.when(jnp.logical_not(there))
        def _():
            tags[slot] = jnp.full(tags.shape[1:], -2, jnp.int32)
    pres[...] = jnp.full(pres.shape, OUT, jnp.float32)
    qacc[...] = jnp.full(qacc.shape, OUT, jnp.float32)

    def normalise(t):
        load(t).wait()
        values = raw[part(t), :].astype(jnp.float32)
        scale = lax.rsqrt(jnp.sum(values * values, axis=1, keepdims=True) + 1e-06)
        blk[OWN, part(t), :] = (values * scale).astype(jnp.bfloat16)

    normalise(order(A, 0, chunks))
    load_ids.wait()
    load_keep.wait()
    tags[OWN, chunks:2 * chunks] = jnp.where(tags[OWN, chunks:2 * chunks] == 1, tags[OWN, 0:chunks], -1)
    heard = sum(there.astype(jnp.int32) for there, _ in partners)
    heard = heard + over_first.astype(jnp.int32) + over_y.astype(jnp.int32) * (2 * crossings - 1)
    heard = heard + (up_l | up_mid).astype(jnp.int32) + up_y.astype(jnp.int32) * (crossings - 1)
    heard = heard - is_r.astype(jnp.int32)

    @pl.when(jnp.logical_not(is_r))
    def _():
        pl.semaphore_wait(barrier, heard)

    @pl.when(above_r)
    def _():
        pl.semaphore_signal(early, inc=1, device_id=device(place - 2), device_id_type=MESH)

    @pl.when(is_r)
    def _():
        pl.semaphore_wait(early, 1)

    @pl.when(over_y)
    def _():
        for i in range(1, crossings):
            pl.semaphore_signal(ready, inc=1, device_id=device(2 * PLANE * (i + 1) + 1), device_id_type=MESH)

    first_now, second_now = has_first & jnp.logical_not(is_r & even), has_second & jnp.logical_not(is_r & odd)

    @pl.when(first_now)
    def _():
        send(A, 0).start()
        send_tags(OWN, A, first).start()

    @pl.when(second_now)
    def _():
        send_tags(OWN, B, second).start()

    def prepare(t, _):
        normalise(order(A, t, chunks))

        @pl.when(first_now)
        def _():
            send(A, t).start()

        return 0

    lax.fori_loop(1, chunks, prepare, 0)

    @pl.when(odd & jnp.logical_not(is_r))
    def _():
        for t in range(chunks):
            send(C, t).start()

    def row(slot, t):
        return tags[slot, pl.ds(t, 1), :]

    def columns(values):
        return jnp.broadcast_to(values, (LANES, LANES)).T

    def fold(values):
        return jnp.max(values.reshape(values.shape[0] // 8, 8, LANES), axis=0)

    def scores(p, q_slot, g):
        q = blk[q_slot, group_at(g), :]
        return lax.dot_general(p, q, (((1,), (1,)), ((), ())), preferred_element_type=jnp.float32)

    def own_step(t, _):
        p = blk[OWN, group_at(t), :]
        labels = jnp.concatenate(
            [columns(row(OWN, chunks + 2 * t + i).astype(jnp.float32)) for i in range(2)], axis=0)
        down = lax.broadcasted_iota(jnp.int32, (2 * LANES, LANES), 0) + t * 2 * LANES
        along = lax.broadcasted_iota(jnp.int32, (2 * LANES, LANES), 1)
        for n in range(chunks // 2):
            s = scores(p, OWN, n)
            for h in range(2):
                tile = 2 * n + h
                ids = row(OWN, tile).astype(jnp.float32)
                hits = (labels == ids) & (down != along + tile * LANES)
                top = fold(jnp.where(hits, s[:, h * LANES:(h + 1) * LANES], OUT))
                at = (0, slice(None), slice(tile * LANES, (tile + 1) * LANES))
                qacc[at] = jnp.maximum(qacc[at], top)
        return 0

    def shared(slot):
        low, high = tags[slot, 0:1, 0:1], tags[slot, chunks - 1:chunks, LANES - 1:LANES]
        if slot == C:
            return low
        return jnp.where(core == (0 if slot == A else 1), low, high)

    def biases(p_slot, t, size, cluster):
        each = [columns(jnp.where(row(p_slot, chunks + t + i) == cluster, 0.0, OUT)) for i in range(size)]
        return jnp.concatenate(each, axis=0) if size > 1 else each[0]

    def tile_pair(p, p_bias, best, q_slot, g, cluster, q_at):
        s = scores(p, q_slot, g)
        for h in range(2):
            one = s[:, h * LANES:(h + 1) * LANES]
            q_bias = jnp.where(row(q_slot, chunks + 2 * g + h) == cluster, 0.0, OUT)
            best = jnp.maximum(best, one + q_bias)
            at = (q_at, slice(None), part(2 * g + h))
            qacc[at] = jnp.maximum(qacc[at], fold(one + p_bias))
        return best

    def keep_rows(p_slot, t, size, best):
        for i in range(size):
            at = (p_slot - 1, slice(None), part(t + i))
            pres[at] = jnp.maximum(pres[at], fold(best[i * LANES:(i + 1) * LANES].T))

    def whole(p_slot, t, size, q_slot, cluster, q_at):
        p = blk[p_slot, pl.ds(pl.multiple_of(t * LANES, LANES), size * LANES), :]
        p_bias = biases(p_slot, t, size, cluster)
        best = jnp.full((size * LANES, LANES), OUT, jnp.float32)
        for g in range(groups):
            best = tile_pair(p, p_bias, best, q_slot, g, cluster, q_at)
        keep_rows(p_slot, t, size, best)

    def some(p_slot, t, size, q_slot, arrivals, cluster, q_at):
        p = blk[p_slot, pl.ds(pl.multiple_of(t * LANES, LANES), size * LANES), :]
        p_bias = biases(p_slot, t, size, cluster)
        best = jnp.full((size * LANES, LANES), OUT, jnp.float32)
        for i in arrivals:
            best = tile_pair(p, p_bias, best, q_slot, order(q_slot, i, groups), cluster, q_at)
        keep_rows(p_slot, t, size, best)

    over_target = device(jnp.where(even, jnp.where(up_last, place - 2 * PLANE, 0), jnp.where(crossing == 0, place + 2 * PLANE, count - 1)))

    def l_at(i):
        return device(2 * (PLANE * (i + 1) - 1) + core)

    def r_at(i):
        return device(2 * PLANE * (i + 1) + core)

    def over(total, i, t, way, target):
        source, there = way
        rows_of = part(order(B, chunks - total + t, chunks))
        return pltpu.make_async_remote_copy(
            src_ref=relay.at[i, t] if source is relay else blk.at[OWN, rows_of],
            dst_ref=relay.at[i, t] if there is relay else blk.at[B, rows_of],
            send_sem=over_send.at[i, t],
            recv_sem=over_recv.at[i, t] if there is relay else recv_sem.at[B, chunks - total + t],
            device_id=target, device_id_type=MESH)

    @pl.when(up_l)
    def _():
        for t in range(UP):
            over(UP, crossing, t, (OWN, relay), over_target).start()

    @pl.when(is_r)
    def _():
        pl.semaphore_wait(barrier, heard)

    @pl.when(is_r & even)
    def _():
        send_tags(OWN, A, first).start()
        for t in range(chunks):
            send(A, t).start()

    @pl.when(is_r & odd)
    def _():
        send_tags(OWN, B, second).start()
        for t in range(chunks):
            send(C, t).start()

    @pl.when(over_first)
    def _():
        for t in range(DOWN):
            over(DOWN, crossing, t, (OWN, relay), over_target).start()


    lax.fori_loop(0, groups, own_step, 0)

    @pl.when(over_to_y)
    def _():
        pl.semaphore_wait(ready, 1)
        for t in range(DOWN):
            over(DOWN, crossing, t, (OWN, relay), over_target).start()

    @pl.when(up_pass)
    def _():
        for t in range(UP):
            over(UP, 2, t, (OWN, relay), first).wait_recv()
            over(UP, 2, t, (relay, relay), over_target).start()

    @pl.when(over_next)
    def _():
        for t in range(DOWN):
            over(DOWN, 0, t, (OWN, relay), first).wait_recv()
            over(DOWN, 0, t, (relay, relay), over_target).start()

    @pl.when(has_first)
    def _():
        for t in range(LEAD):
            send(A, t).wait_send()

    @pl.when(is_r & odd)
    def _():
        for t in range(LEAD, LEAD + MORE):
            send(A, t).wait_send()

    @pl.when(has_second)
    def _():
        for t in range(chunks - DOWN):
            send(B, t).start()

    @pl.when(has_second & jnp.logical_not(over_r))
    def _():
        for t in range(chunks - DOWN, chunks - UP):
            send(B, t).start()

    @pl.when(has_second & jnp.logical_not(over_r | up_l))
    def _():
        for t in range(chunks - UP, chunks):
            send(B, t).start()

    @pl.when(has_first)
    def _():
        send_tags(OWN, A, first).wait_send()

    @pl.when(has_second)
    def _():
        send_tags(OWN, B, second).wait_send()

    @pl.when(has_a)
    def _():
        send_tags(OWN, A, first).wait_recv()

    @pl.when(has_b)
    def _():
        send_tags(OWN, B, second).wait_recv()

    @pl.when(gives_c)
    def _():
        send_tags(c_source, C, sibling).start()
        send_tags(c_source, C, sibling).wait_send()

    @pl.when(has_c)
    def _():
        send_tags(c_source, C, sibling).wait_recv()

    s_a, s_b, s_c = shared(A), shared(B), shared(C)

    @pl.when(even)
    def _():
        for t in range(chunks):
            send(C, t).wait_recv()

    def edge_copies():
        return (
            pltpu.make_async_remote_copy(
                src_ref=blk.at[A, part(0)], dst_ref=edge_rows, send_sem=edge_send.at[0], recv_sem=edge_recv.at[0],
                device_id=first, device_id_type=MESH),
            pltpu.make_async_remote_copy(
                src_ref=tags.at[A], dst_ref=edge_tags, send_sem=edge_send.at[1], recv_sem=edge_recv.at[1],
                device_id=first, device_id_type=MESH))

    def edge_message():
        return pltpu.make_async_remote_copy(
            src_ref=edge_out, dst_ref=edge_got, send_sem=edge_send.at[2], recv_sem=edge_recv.at[2],
            device_id=second, device_id_type=MESH)

    def step(j, _):
        @pl.when(up_mid & (j == groups - 1))
        def _():
            for t in range(UP):
                over(UP, 1, t, (OWN, relay), first).wait_recv()
                over(UP, 1, t, (relay, B), r_at(1)).start()

        @pl.when(over_y & (j == groups - 3))
        def _():
            for i in range(crossings):
                for t in range(DOWN):
                    over(DOWN, i, t, (OWN, relay), first).wait_recv()
                    over(DOWN, i, t, (relay, B), l_at(i)).start()

        @pl.when(up_y & (j == groups - 2))
        def _():
            for i in (1, 0, 2):
                for t in range(UP):
                    over(UP, i, t, (OWN, relay), first).wait_recv()
                    over(UP, i, t, (relay, relay if i == 1 else B), r_at(0 if i == 1 else i)).start()

        @pl.when(has_a)
        def _():
            send(A, 2 * j).wait_recv()
            send(A, 2 * j + 1).wait_recv()

        @pl.when(even & has_a)
        def _():
            send(C, 2 * j).start()
            send(C, 2 * j + 1).start()

        @pl.when(up_l & (j == 0))
        def _():
            for each in edge_copies():
                each.start()

        @pl.when(has_a)
        def _():
            whole(A, 2 * order(A, j, groups), 2, OWN, s_a, 1)

        @pl.when(odd & has_c)
        def _():
            send(C, 2 * j).wait_recv()
            send(C, 2 * j + 1).wait_recv()

        @pl.when(has_c)
        def _():
            whole(C, 2 * j, 2, OWN, s_c, 2)

        for now in range(groups):
            @pl.when(odd & has_a & has_c & (j == now))
            def _():
                some(C, 2 * now, 2, A, range(now + 1), s_c, 4)
                if now > 0:
                    some(A, 2 * order(A, now, groups), 2, C, range(now), s_a, 5)

        m = j - 1

        @pl.when(has_b & (j > 0) & (j < groups - 1))
        def _():
            send(B, 2 * m).wait_recv()
            send(B, 2 * m + 1).wait_recv()

            @pl.when(even)
            def _():
                whole(B, 2 * order(B, m, groups), 2, C, s_b, 4)

            for now in range(groups - 2):
                @pl.when(has_a & (m == now))
                def _():
                    some(B, 2 * order(B, now, groups), 2, A, range(min(now + 2, groups - now)), s_b, 3)

        return 0

    lax.fori_loop(0, groups, step, 0)

    def message(which, target):
        return pltpu.make_async_remote_copy(
            src_ref=msg.at[which], dst_ref=got.at[which], send_sem=msg_send.at[which],
            recv_sem=msg_recv.at[which], device_id=target, device_id_type=MESH)

    def masked(slot, tile, cluster, values):
        return jnp.where(row(slot, tile) == cluster, jnp.max(values, axis=0, keepdims=True), -1.0)

    def message_a(tile):
        msg[0, pl.ds(tile, 1), :] = jnp.maximum(
            jnp.maximum(masked(A, tile, s_a, pres[0, :, part(tile)]), masked(A, tile, s_b, qacc[3, :, part(tile)])),
            jnp.where(odd, masked(A, tile, s_c, qacc[4, :, part(tile)]), -1.0))

    def message_b(tile):
        msg[1, pl.ds(tile, 1), :] = masked(B, tile, s_b, pres[1, :, part(tile)])

    for tile in range(chunks):
        msg[2, tile:tile + 1, :] = jnp.maximum(
            masked(C, tile, s_c, pres[2, :, part(tile)]), jnp.where(odd, masked(C, tile, s_a, qacc[5, :, part(tile)]), -1.0))

    @pl.when(odd & has_c)
    def _():
        message(2, above).start()

    for tile in range(chunks):
        own = jnp.max(qacc[0, :, part(tile)], axis=0, keepdims=True)
        out_ref[tile:tile + 1, :] = jnp.maximum(
            jnp.maximum(own, -1.0),
            jnp.maximum(masked(OWN, tile, s_a, qacc[1, :, part(tile)]), masked(OWN, tile, s_c, qacc[2, :, part(tile)])))

    @pl.when(edge)
    def _():
        for each in edge_copies():
            each.wait_recv()
        cluster = edge_tags[0:1, 0:1]
        s = lax.dot_general(
            edge_rows[...], blk[OWN, part(0), :], (((1,), (1,)), ((), ())), preferred_element_type=jnp.float32)
        p_bias = columns(jnp.where(edge_tags[chunks:chunks + 1, :] == cluster, 0.0, OUT))
        q_bias = jnp.where(row(OWN, chunks) == cluster, 0.0, OUT)
        rows_best = jnp.max((s + q_bias).T, axis=0, keepdims=True)
        edge_out[...] = jnp.broadcast_to(jnp.where(edge_tags[0:1, :] == cluster, rows_best, -1.0), edge_out.shape)
        edge_message().start()
        own_best = jnp.max(s + p_bias, axis=0, keepdims=True)
        out_ref[0:1, :] = jnp.maximum(out_ref[0:1, :], jnp.where(row(OWN, 0) == cluster, own_best, -1.0))

    @pl.when(has_a & has_b)
    def _():
        some(B, 2 * order(B, 0, groups), 2, A, range(2, groups), s_b, 3)

    for t in range(4, chunks):
        message_a(order(A, t, chunks))
    for t in range(chunks - 4):
        message_b(order(B, t, chunks))

    @pl.when(over_l)
    def _():
        for t in range(chunks - 2, chunks):
            send(B, t).wait_recv()
        some(B, 2 * order(B, groups - 1, groups), 2, A, range(1), s_b, 3)
        for t in range(chunks - 2, chunks):
            message_b(order(B, t, chunks))

    @pl.when(has_b)
    def _():
        m = groups - 2
        send(B, 2 * m).wait_recv()
        send(B, 2 * m + 1).wait_recv()

        @pl.when(has_a)
        def _():
            some(B, 2 * order(B, m, groups), 2, A, range(groups - m), s_b, 3)

        @pl.when(even)
        def _():
            whole(B, 2 * order(B, m, groups), 2, C, s_b, 4)

    for t in range(chunks - 4, chunks - 2):
        message_b(order(B, t, chunks))

    @pl.when(over_l)
    def _():
        message(1, first).start()

    for t in range(2, 4):
        message_a(order(A, t, chunks))

    def last_step(i, _):
        t = i + up_r.astype(jnp.int32) * (2 * chunks - 3 - 2 * i)

        comes = has_b & jnp.logical_not(over_l)

        @pl.when(comes)
        def _():
            send(B, t).wait_recv()

        @pl.when(up_r)
        def _():
            whole(B, order(B, t, chunks), 1, C, s_b, 4)

        @pl.when(up_r & (i == chunks - 1))
        def _():
            for tile in range(chunks):
                msg[2, tile:tile + 1, :] = jnp.maximum(
                    msg[2, tile:tile + 1, :], masked(C, tile, s_b, qacc[4, :, part(tile)]))
            message(2, above).start()

        @pl.when(has_a & comes)
        def _():
            some(B, order(B, t, chunks), 1, A, range(1), s_b, 3)

        @pl.when(odd & comes)
        def _():
            message_b(order(B, t, chunks))

        @pl.when(odd & comes & (i == chunks - 1))
        def _():
            message(1, first).start()

        @pl.when(i == jnp.where(up_l, chunks - 2, chunks - 1))
        def _():
            for each in range(2):
                message_a(order(A, each, chunks))

            @pl.when(up_l)
            def _():
                edge_message().wait_recv()
                msg[0, 0:1, :] = jnp.maximum(msg[0, 0:1, :], edge_got[0:1, :])

            @pl.when(has_a)
            def _():
                message(0, second).start()

        @pl.when(even & has_b & jnp.logical_not(up_r))
        def _():
            whole(B, order(B, t, chunks), 1, C, s_b, 4)

        @pl.when(even & has_b)
        def _():
            message_b(order(B, t, chunks))

        return 0

    lax.fori_loop(chunks - 2, chunks, last_step, 0)

    @pl.when(even & has_b)
    def _():
        message(1, first).start()

    @pl.when(even & jnp.logical_not(up_r))
    def _():
        for tile in range(chunks):
            msg[2, tile:tile + 1, :] = jnp.maximum(
                msg[2, tile:tile + 1, :], masked(C, tile, s_b, qacc[4, :, part(tile)]))
        message(2, above).start()

    messages = ((has_a, second, has_first), (has_b, first, has_second), (has_c, above, odd | has_down))
    @pl.when(has_first)
    def _():
        for t in range(LEAD + MORE, chunks):
            send(A, t).wait_send()

    @pl.when(has_first & jnp.logical_not(is_r & odd))
    def _():
        for t in range(LEAD, LEAD + MORE):
            send(A, t).wait_send()

    @pl.when(has_second)
    def _():
        for t in range(chunks - DOWN):
            send(B, t).wait_send()

    @pl.when(has_second & jnp.logical_not(over_r))
    def _():
        for t in range(chunks - DOWN, chunks - UP):
            send(B, t).wait_send()

    @pl.when(has_second & jnp.logical_not(over_r | up_l))
    def _():
        for t in range(chunks - UP, chunks):
            send(B, t).wait_send()

    @pl.when(over_r)
    def _():
        for t in range(DOWN):
            over(DOWN, crossing, t, (OWN, relay), over_target).wait_send()

    @pl.when(over_next)
    def _():
        for t in range(DOWN):
            over(DOWN, 0, t, (relay, relay), over_target).wait_send()

    @pl.when(over_y)
    def _():
        for i in range(crossings):
            for t in range(DOWN):
                over(DOWN, i, t, (relay, B), l_at(i)).wait_send()

    @pl.when(up_l)
    def _():
        for t in range(UP):
            over(UP, crossing, t, (OWN, relay), over_target).wait_send()

    @pl.when(up_pass)
    def _():
        for t in range(UP):
            over(UP, 2, t, (relay, relay), over_target).wait_send()

    @pl.when(up_mid)
    def _():
        for t in range(UP):
            over(UP, 1, t, (relay, B), r_at(1)).wait_send()

    @pl.when(up_y)
    def _():
        for i in range(crossings):
            for t in range(UP):
                over(UP, i, t, (relay, relay if i == 1 else B), r_at(0 if i == 1 else i)).wait_send()

    @pl.when(gives_c)
    def _():
        for t in range(chunks):
            send(C, t).wait_send()

    @pl.when(up_l)
    def _():
        for each in edge_copies():
            each.wait_send()

    @pl.when(edge)
    def _():
        edge_message().wait_send()

    for which, (gives, target, gets) in enumerate(messages):
        @pl.when(gives)
        def _():
            message(which, target).wait_send()

        @pl.when(gets)
        def _():
            message(which, target).wait_recv()
            out_ref[...] = jnp.maximum(out_ref[...], got[which])


def shards(n_slab, n_member, embeddings, cluster_ids, keep_mask):
    rows, width = embeddings.shape
    chunks = rows // LANES
    crossings = n_slab * n_member // 2 // PLANE - 1
    highest = pl.pallas_call(
        functools.partial(kernel, n_slab, n_member),
        out_shape=jax.ShapeDtypeStruct((chunks, LANES), jnp.float32),
        in_specs=[pl.BlockSpec(memory_space=pltpu.HBM)] * 3,
        out_specs=pl.BlockSpec(memory_space=pltpu.VMEM),
        scratch_shapes=[
            pltpu.VMEM((rows, width), jnp.bfloat16),
            pltpu.VMEM((4, rows, width), jnp.bfloat16),
            pltpu.VMEM((4, 2 * chunks, LANES), jnp.int32),
            pltpu.VMEM((3, 8, rows), jnp.float32),
            pltpu.VMEM((6, 8, rows), jnp.float32),
            pltpu.VMEM((3, chunks, LANES), jnp.float32),
            pltpu.VMEM((3, chunks, LANES), jnp.float32),
            pltpu.VMEM((crossings, DOWN, LANES, width), jnp.bfloat16),
            pltpu.SemaphoreType.DMA((chunks + 2,)),
            pltpu.SemaphoreType.DMA((4, chunks)),
            pltpu.SemaphoreType.DMA((4, chunks)),
            pltpu.SemaphoreType.DMA((4,)),
            pltpu.SemaphoreType.DMA((4,)),
            pltpu.SemaphoreType.DMA((3,)),
            pltpu.SemaphoreType.DMA((3,)),
            pltpu.SemaphoreType.DMA((crossings, DOWN)),
            pltpu.SemaphoreType.DMA((crossings, DOWN)),
            pltpu.SemaphoreType.REGULAR,
            pltpu.SemaphoreType.REGULAR,
            pltpu.VMEM((LANES, width), jnp.bfloat16),
            pltpu.VMEM((2 * chunks, LANES), jnp.int32),
            pltpu.VMEM((8, LANES), jnp.float32),
            pltpu.VMEM((8, LANES), jnp.float32),
            pltpu.SemaphoreType.DMA((3,)),
            pltpu.SemaphoreType.DMA((3,)),
        ],
        compiler_params=pltpu.CompilerParams(
            collective_id=0, has_side_effects=True, vmem_limit_bytes=40 << 20),
    )(*(pltpu.with_memory_space_constraint(each, pltpu.HBM) for each in (
        embeddings, cluster_ids.reshape(chunks, LANES), keep_mask.reshape(chunks, LANES))))
    return highest.reshape(rows)


def solution(mesh):
    placed = (P(("slab", "member"), None), P(("slab", "member")), P(("slab", "member")))
    return jax.shard_map(
        functools.partial(shards, mesh.shape["slab"], mesh.shape["member"]),
        mesh=mesh, in_specs=placed, out_specs=P(("slab", "member")), check_vma=False,
    )
```
